256 devices in a mesh: dp: 16 (over x, y), ctx: 16 (over z, core).
Axes of the slice: x: 4, y: 4, z: 8, core: 2. Of those that a mesh axis runs over, the one named last changes fastest.
Arguments:
- frames: bfloat16 [512, 256, 1408], P(('dp', 'ctx')), may hold values from -6 to 6
- cotangent: bfloat16 [512, 256, 1408], P(('dp', 'ctx')), may hold values from -6 to 6
- clip_ids: int32 [16, 32], P('dp'), may hold values from 0 to 2, never falling along the last dimension, each value on 1 to 24 neighbouring positions
- gain: float32 [1408], replicated, may hold values from 0.1 to 1.9
- query_key_value_weight: bfloat16 [1408, 2112], replicated, may hold values from -4 to 4
- w_out: bfloat16 [704, 1408], replicated, may hold values from -0.21875 to 0.21875
Outputs:
- frame_input_gradient: bfloat16 [512, 256, 1408], P(('dp', 'ctx'))
- gain_grad: float32 [1408], replicated
The draws below stay inside these ranges and needn't reach their ends.
Inputs may be any that keep to these rules, and one draw needn't show every extreme that they name: `clip_ids`: in each row (one group of 32 frames) ids never fall; each of the 3 clips holds 1 to 24 consecutive frames and one holds exactly 24.
All inputs are finite; a program needn't handle non-finite values.
Results may differ from the reference program's by a relative error of at most 0.005.
The reference program's roundings to bfloat16 on the way count: a program that leaves them out, or rounds other values in their place, can miss the bound.
Values may be sent and summed in bfloat16 or wider, within the bound.
No kernel may reach another device: no remote copies, remote signals or barrier semaphores. Data moves between devices by JAX's collectives and lax.ppermute only.
A program may use at most 64 MiB of HBM per device.

```python
import math
import jax
import jax.numpy as jnp
import numpy as np
from jax import lax

D = 1408
HEADS = 8
PATCHES = 256
CLIPS = 3
INNER = 704
GROUPS = 16
GROUP_FRAMES = 32
CLIP_MOST = 24
FRAMES = 512
N_DP = 16


def draw_frames(key, part):
    key = jax.random.fold_in(key, 11)
    second_term = jax.random.fold_in(key, 1)
    return jnp.clip(jax.random.normal(second_term, (FRAMES, PATCHES, D), jnp.float32), -6.0, 6.0).astype(jnp.bfloat16)


def draw_query_key_value_weight(key, part):
    key = jax.random.fold_in(key, 23)
    first_term = jax.random.fold_in(key, 0)
    base = jnp.clip(jax.random.normal(first_term, (D, 3 * INNER), jnp.float32), -6.0, 6.0) / jnp.sqrt(jnp.float32(D))
    return base.astype(jnp.bfloat16)


def shard_levels(own_key, shape, cuts, low, high):
    factor_of = 1.0
    for dim, blocks in cuts:
        heights = jax.random.uniform(jax.random.fold_in(jax.random.fold_in(own_key, 6), dim), (blocks,), jnp.float32, low / len(cuts), high / len(cuts))
        factor_of = factor_of * jnp.repeat(jnp.exp(heights), shape[dim] // blocks).reshape((-1,) + (1,) * (len(shape) - 1 - dim))
    return factor_of


def split_up(number_of, total, limit, slope):
    loads = [(1 << 20) // math.isqrt(rank ** slope) + 1 for rank in range(2, number_of + 1)]
    surplus, counts = total - limit - (number_of - 1), [1] * (number_of - 1)
    while surplus > 0:
        candidates = [i for i in range(number_of - 1) if counts[i] < limit]
        whole, remaining = sum([loads[i] for i in candidates]), surplus
        for i in candidates:
            extra = min(limit - counts[i], max(1, remaining * loads[i] // whole), surplus)
            counts[i] = counts[i] + extra
            surplus = surplus - extra
    return np.array([limit] + counts)


def uneven_parts(own_key, number_of, total, bound, slope):
    if number_of == 2:
        one = jax.random.randint(own_key, (), max(1, total - bound), min(bound, total - 1) + 1)
        return jnp.stack([one, total - one])
    sizes = jnp.asarray(split_up(number_of, total, bound, slope), jnp.int32)
    couples = (number_of - 1) // 2
    donor, taker = sizes[1:1 + 2 * couples:2], sizes[2:2 + 2 * couples:2]
    margin = jnp.minimum(donor - 1, bound - taker)
    shifted = jax.random.randint(jax.random.fold_in(own_key, 1), (couples,), 0, 1 << 20) % (margin + 1)
    sizes = sizes.at[1:1 + 2 * couples:2].set(donor - shifted).at[2:2 + 2 * couples:2].set(taker + shifted)
    return sizes[jax.random.permutation(jax.random.fold_in(own_key, 2), number_of)]


def scatter_about(rng, dims, width, limit, pieces=(), held_as=jnp.bfloat16):
    level = shard_levels(rng, dims, pieces, -0.22, 0.18) if pieces else 1.0
    entries = jax.random.normal(rng, dims, jnp.float32) * width * level
    return jnp.minimum(jnp.maximum(entries, -limit), limit).astype(held_as)


def setup_inputs(seed: int = 0) -> dict:
    splits = jax.random.split(jax.random.key(seed), 7)
    return {
        "frames": draw_frames(jax.random.fold_in(splits[6], 71), 0),
        "cotangent": scatter_about(splits[1], (FRAMES, PATCHES, D), 1.0, 6.0, ((0, 256),)),
        "clip_ids": jax.vmap(lambda own: jnp.searchsorted(jnp.cumsum(uneven_parts(own, CLIPS, GROUP_FRAMES, CLIP_MOST, 2)), jnp.arange(GROUP_FRAMES), side="right"))(jax.random.split(splits[2], GROUPS)).reshape((GROUPS, GROUP_FRAMES)).astype(jnp.int32),
        "gain": jnp.clip(1.0 + 0.18 * jax.random.normal(splits[3], (D,), jnp.float32), 0.1, 1.9),
        "query_key_value_weight": draw_query_key_value_weight(jax.random.fold_in(splits[6], 71), 0),
        "w_out": scatter_about(splits[5], (INNER, D), INNER ** -0.5, 0.21875),
    }


def apply_norm(frames, gain):
    values = frames.astype(jnp.float32)
    centered_values = values - lax.optimization_barrier(jnp.mean(values, axis=-1, keepdims=True))
    inverse_deviation = lax.rsqrt(lax.optimization_barrier(jnp.mean(centered_values * centered_values, axis=-1, keepdims=True)) + 1e-05)
    standardized_input = centered_values * inverse_deviation
    return ((standardized_input * gain.astype(jnp.float32)).astype(jnp.bfloat16), standardized_input, inverse_deviation)

def norm_backward(normed_gradient, standardized_input, inverse_deviation, gain):
    expanded_values = normed_gradient * gain.astype(jnp.float32)
    first_term = lax.optimization_barrier(jnp.mean(expanded_values, axis=-1, keepdims=True))
    second_term = lax.optimization_barrier(jnp.mean(expanded_values * standardized_input, axis=-1, keepdims=True))
    return inverse_deviation * (expanded_values - first_term - standardized_input * second_term)

def split_heads(block, heads):
    return block.reshape(block.shape[0], block.shape[1], heads, -1).astype(jnp.float32)

def attend(query_key_value, same, heads):
    inner = query_key_value.shape[-1] // 3
    query = split_heads(query_key_value[..., :inner], heads)
    keys = split_heads(query_key_value[..., inner:2 * inner], heads)
    scale = 1.0 / math.sqrt(inner // heads)
    scores = jnp.einsum('fphd,gphd->phfg', query, keys) * scale
    scores = jnp.where(same, scores, -1e+30)
    top = lax.optimization_barrier(jnp.max(scores, axis=-1, keepdims=True))
    expo = jnp.exp(scores - top)
    probs = expo / lax.optimization_barrier(jnp.sum(expo, axis=-1, keepdims=True))
    weights = probs.astype(jnp.bfloat16)
    return (probs, weights)

def attend_back(query_key_value, probs, weights, d_attn, heads):
    inner = query_key_value.shape[-1] // 3
    query = split_heads(query_key_value[..., :inner], heads)
    keys = split_heads(query_key_value[..., inner:2 * inner], heads)
    value = split_heads(query_key_value[..., 2 * inner:], heads)
    scale = 1.0 / math.sqrt(inner // heads)
    d_heads = split_heads(d_attn, heads)
    d_weights = jnp.einsum('fphd,gphd->phfg', d_heads, value)
    d_value = jnp.einsum('phfg,fphd->gphd', weights.astype(jnp.float32), d_heads)
    d_scores = probs * (d_weights - lax.optimization_barrier(jnp.sum(probs * d_weights, axis=-1, keepdims=True)))
    d_scores = d_scores.astype(jnp.bfloat16).astype(jnp.float32)
    d_query = jnp.einsum('phfg,gphd->fphd', d_scores, keys) * scale
    d_key = jnp.einsum('phfg,fphd->gphd', d_scores, query) * scale
    lead = (query_key_value.shape[0], query_key_value.shape[1], inner)
    joined = jnp.concatenate([d_query.reshape(lead), d_key.reshape(lead), d_value.reshape(lead)], axis=-1)
    return joined.astype(jnp.bfloat16)

def group_pass(frames, cotangent, clip_row, gain, query_key_value_weight, w_out):
    normalized_frames, standardized_input, inverse_deviation = apply_norm(frames, gain)
    lead = frames.shape[:2]
    query_key_value = jnp.dot(normalized_frames.reshape(-1, frames.shape[2]), query_key_value_weight, preferred_element_type=jnp.float32)
    query_key_value = query_key_value.astype(jnp.bfloat16).reshape(lead + (query_key_value_weight.shape[1],))
    same = clip_row[:, None] == clip_row[None, :]
    probs, weights = attend(query_key_value, same, HEADS)
    d_attn = jnp.dot(cotangent.reshape(-1, frames.shape[2]), w_out.T, preferred_element_type=jnp.float32)
    d_attn = d_attn.astype(jnp.bfloat16).reshape(lead + (w_out.shape[0],))
    query_key_value_gradient = attend_back(query_key_value, probs, weights, d_attn, HEADS)
    normed_gradient = jnp.dot(query_key_value_gradient.reshape(-1, query_key_value_gradient.shape[2]), query_key_value_weight.T, preferred_element_type=jnp.float32)
    normed_gradient = normed_gradient.reshape(frames.shape)
    frame_input_gradient = (cotangent.astype(jnp.float32) + norm_backward(normed_gradient, standardized_input, inverse_deviation, gain)).astype(jnp.bfloat16)
    partial_term = lax.optimization_barrier(jnp.sum((normed_gradient * standardized_input).reshape(-1, frames.shape[2]), axis=0))
    return (frame_input_gradient, partial_term)

def reference(frames, cotangent, clip_ids, gain, query_key_value_weight, w_out):
    grouped = frames.reshape(N_DP, -1, PATCHES, D)
    grouped_cot = cotangent.reshape(N_DP, -1, PATCHES, D)

    def step(total, items):
        frame_input_gradient, partial_term = group_pass(items[0], items[1], items[2], gain, query_key_value_weight, w_out)
        return (total + partial_term, frame_input_gradient)
    start = jnp.zeros((D,), jnp.float32)
    total, grads = lax.scan(step, start, (grouped, grouped_cot, clip_ids))
    return (grads.reshape(frames.shape), total * (1.0 / math.sqrt(FRAMES * PATCHES)))
```

```python
import functools
import math

import jax
import jax.numpy as jnp
from jax import lax
from jax.experimental import pallas as pl
from jax.experimental.pallas import tpu as pltpu
from jax.sharding import PartitionSpec as P

HEADS = 8
HALF = 8
VMEM_BYTES = 48 * 1024 * 1024


def dot_nn(a, b):
    return lax.dot_general(a, b, (((1,), (0,)), ((), ())), preferred_element_type=jnp.float32)


def dot_nt(a, b):
    return lax.dot_general(a, b, (((1,), (1,)), ((), ())), preferred_element_type=jnp.float32)


def dot_tn(a, b):
    return lax.dot_general(a, b, (((0,), (0,)), ((), ())), preferred_element_type=jnp.float32)


def standardize(block):
    values = block.astype(jnp.float32)
    centered = values - jnp.mean(values, axis=-1, keepdims=True)
    inverse = lax.rsqrt(jnp.mean(centered * centered, axis=-1, keepdims=True) + 1e-05)
    return centered * inverse, inverse


def project_kernel(x_ref, gain_ref, w_ref, qkv_ref, normed):
    frames, patches, d = x_ref.shape
    inner = w_ref.shape[1] // 3
    wide = qkv_ref.shape[1] // 3
    rows = frames * HALF
    step = 4

    def norm_step(i, carry):
        xhat, _ = standardize(x_ref[pl.ds(i * step, step)])
        scaled = xhat * gain_ref[...].reshape(1, 1, d)
        for half in range(patches // HALF):
            part = scaled[:, half * HALF : (half + 1) * HALF, :].reshape(step * HALF, d)
            at = pl.multiple_of(half * rows + i * step * HALF, step * HALF)
            normed[pl.ds(at, step * HALF), :] = part.astype(jnp.bfloat16)
        return carry

    lax.fori_loop(0, frames // step, norm_step, 0)
    for block in range(frames * patches // rows):
        piece = slice(block * rows, (block + 1) * rows)
        joined = dot_nn(normed[piece, :], w_ref[...]).astype(jnp.bfloat16)
        for part in range(3):
            qkv_ref[piece, part * wide : part * wide + inner] = joined[:, part * inner : (part + 1) * inner]
            qkv_ref[piece, part * wide + inner : (part + 1) * wide] = jnp.zeros(
                (rows, wide - inner), jnp.bfloat16
            )


def attend_kernel(
    qkv_ref, d_ref, x_ref, column_ref, row_ref, gain_ref, w_ref, out_ref, partial_ref,
    bias, d_attn, d_query, d_key, d_value, joined, d_norm,
):
    frames, patches, d = x_ref.shape
    inner = w_ref.shape[1] // 3
    wide = qkv_ref.shape[1] // 3
    head = inner // HEADS
    rows = frames * HALF
    halves = patches // HALF
    scale = 1.0 / math.sqrt(head)
    bias[...] = jnp.where(column_ref[...] == row_ref[...], 0.0, -1e30)
    d_attn[:, inner:] = jnp.zeros((halves * rows, wide - inner), jnp.bfloat16)
    step = 4

    def split_step(i, carry):
        block = d_ref[pl.ds(i * step, step)].astype(jnp.float32)
        for half in range(halves):
            part = block[:, half * HALF : (half + 1) * HALF, :].reshape(step * HALF, inner)
            at = pl.multiple_of(half * rows + i * step * HALF, step * HALF)
            d_attn[pl.ds(at, step * HALF), :inner] = part.astype(jnp.bfloat16)
        return carry

    lax.fori_loop(0, frames // step, split_step, 0)

    def half_step(half, carry):
        at = pl.ds(pl.multiple_of(half * rows, rows), rows)
        done = 0
        for h in range(HEADS):
            low = (h * head) // 128 * 128
            high = min(-(-((h + 1) * head) // 128) * 128, wide)
            lanes = lax.broadcasted_iota(jnp.int32, (rows, high - low), 1) + low
            own = (lanes >= h * head) & (lanes < (h + 1) * head)

            def only(block):
                return jnp.where(own, block, jnp.zeros_like(block))

            query = only(qkv_ref[at, low:high])
            key = only(qkv_ref[at, wide + low : wide + high])
            value = qkv_ref[at, 2 * wide + low : 2 * wide + high]
            cot = only(d_attn[at, low:high])
            scores = dot_nt(key, query) * scale + bias[...]
            expo = jnp.exp(scores - jnp.max(scores, axis=0, keepdims=True))
            probs = expo * (1.0 / jnp.sum(expo, axis=0, keepdims=True))
            d_weights = dot_nt(value, cot)
            d_scores = probs * (d_weights - jnp.sum(probs * d_weights, axis=0, keepdims=True))
            d_scores = d_scores.astype(jnp.bfloat16)
            for target, found in (
                (d_query, dot_tn(d_scores, key) * scale),
                (d_key, dot_nn(d_scores, query) * scale),
                (d_value, dot_nn(probs.astype(jnp.bfloat16), cot)),
            ):
                shared = max(done - low, 0)
                if shared:
                    target[:, low:done] += found[:, :shared]
                if high > done:
                    target[:, max(low, done) : high] = found[:, shared:]
            done = high
        joined[at, 0:inner] = d_query[:, :inner].astype(jnp.bfloat16)
        joined[at, inner : 2 * inner] = d_key[:, :inner].astype(jnp.bfloat16)
        joined[at, 2 * inner :] = d_value[:, :inner].astype(jnp.bfloat16)
        d_norm[at, :] = dot_nt(joined[at, :], w_ref[...])
        return carry

    lax.fori_loop(0, halves, half_step, 0)
    partial_ref[...] = jnp.zeros_like(partial_ref)

    def back_step(i, carry):
        xhat, inverse = standardize(x_ref[pl.ds(i * step, step)])
        grads = jnp.concatenate(
            [
                d_norm[
                    pl.ds(pl.multiple_of(half * rows + i * step * HALF, step * HALF), step * HALF), :
                ].reshape(step, HALF, d)
                for half in range(halves)
            ],
            axis=1,
        )
        partial_ref[...] += jnp.sum((grads * xhat).reshape(step * patches, d), axis=0, keepdims=True)
        e = grads * gain_ref[...].reshape(1, 1, d)
        first = jnp.mean(e, axis=-1, keepdims=True)
        second = jnp.mean(e * xhat, axis=-1, keepdims=True)
        out_ref[pl.ds(i * step, step)] = (inverse * (e - first - xhat * second)).astype(jnp.bfloat16)
        return carry

    lax.fori_loop(0, frames // step, back_step, 0)


def vmem(count):
    return [pl.BlockSpec(memory_space=pltpu.VMEM)] * count


def project(x, gain, weight):
    frames, patches, d = x.shape
    inner = weight.shape[1] // 3
    wide = -(-inner // 128) * 128
    rows = frames * patches
    return pl.pallas_call(
        project_kernel,
        out_shape=jax.ShapeDtypeStruct((rows, 3 * wide), jnp.bfloat16),
        in_specs=vmem(3),
        out_specs=vmem(1)[0],
        scratch_shapes=[pltpu.VMEM((rows, d), jnp.bfloat16)],
        compiler_params=pltpu.CompilerParams(vmem_limit_bytes=VMEM_BYTES),
        cost_estimate=pl.CostEstimate(
            flops=2 * rows * d * 3 * inner, bytes_accessed=2 * (rows * d + 3 * inner * (rows + d)), transcendentals=0
        ),
        name="project",
    )(x, gain.reshape(1, d), weight)


def attend(qkv, d_attn, x, clip_row, gain, weight):
    frames, patches, d = x.shape
    inner = weight.shape[1] // 3
    wide = qkv.shape[1] // 3
    rows = frames * HALF
    total = frames * patches
    code = (clip_row[:, None] * HALF + jnp.arange(HALF, dtype=jnp.int32)[None, :]).reshape(rows)
    return pl.pallas_call(
        attend_kernel,
        out_shape=(
            jax.ShapeDtypeStruct(x.shape, jnp.bfloat16),
            jax.ShapeDtypeStruct((1, d), jnp.float32),
        ),
        in_specs=vmem(7),
        out_specs=tuple(vmem(2)),
        scratch_shapes=[
            pltpu.VMEM((rows, rows), jnp.float32),
            pltpu.VMEM((total, wide), jnp.bfloat16),
            pltpu.VMEM((rows, wide), jnp.float32),
            pltpu.VMEM((rows, wide), jnp.float32),
            pltpu.VMEM((rows, wide), jnp.float32),
            pltpu.VMEM((total, 3 * inner), jnp.bfloat16),
            pltpu.VMEM((total, d), jnp.float32),
        ],
        compiler_params=pltpu.CompilerParams(vmem_limit_bytes=VMEM_BYTES),
        cost_estimate=pl.CostEstimate(
            flops=2 * total * d * 3 * inner, bytes_accessed=2 * (total * d + 3 * inner * (total + d)), transcendentals=0
        ),
        name="attend",
    )(qkv, d_attn, x, code.reshape(rows, 1), code.reshape(1, rows), gain.reshape(1, d), weight)


def to_homes(block, members):
    frames, patches, features = block.shape
    own = patches // members
    sent = block.reshape(frames, members, own, features).transpose(1, 0, 2, 3)
    got = lax.all_to_all(sent, "ctx", 0, 0, tiled=True)
    return got.reshape(members * frames, own, features)


def to_frames(block, members):
    frames, own, features = block.shape
    got = lax.all_to_all(block.reshape(members, frames // members, own, features), "ctx", 0, 0, tiled=True)
    return got.transpose(1, 0, 2, 3).reshape(frames // members, members * own, features)


def sum_all(value, mesh_sizes):
    for axis, size in mesh_sizes:
        stride = 1
        while stride < size:
            radix = min(4, size // stride)
            moved = [value]
            for k in range(1, radix):
                pairs = [
                    (i, i - (i // stride % radix) * stride + (i // stride + k) % radix * stride)
                    for i in range(size)
                ]
                moved.append(lax.ppermute(value, axis, pairs))
            value = functools.reduce(jnp.add, moved)
            stride *= radix
    return value


def on_device(frames, cotangent, clip_ids, gain, query_key_value_weight, w_out):
    groups = lax.axis_size("dp")
    members = lax.axis_size("ctx")
    count = groups * members * frames.shape[0] * frames.shape[1]
    x = to_homes(frames, members)
    d_attn = lax.dot_general(
        cotangent.reshape(-1, cotangent.shape[2]),
        w_out,
        (((1,), (1,)), ((), ())),
        preferred_element_type=jnp.float32,
    )
    d_attn = d_attn.astype(jnp.bfloat16).reshape(cotangent.shape[:2] + (w_out.shape[0],))
    d_attn = to_homes(d_attn, members)
    qkv = project(x, gain, query_key_value_weight)
    term, partial_term = attend(qkv, d_attn, x, clip_ids[0], gain, query_key_value_weight)
    back = to_frames(term, members)
    frame_input_gradient = (cotangent.astype(jnp.float32) + back.astype(jnp.float32)).astype(jnp.bfloat16)
    total = sum_all(partial_term[0], (("dp", groups), ("ctx", members)))
    return (frame_input_gradient, total * (1.0 / math.sqrt(count)))


def solution(mesh):
    return jax.shard_map(
        on_device,
        mesh=mesh,
        in_specs=(
            P(("dp", "ctx"), None, None),
            P(("dp", "ctx"), None, None),
            P("dp", None),
            P(),
            P(),
            P(),
        ),
        out_specs=(P(("dp", "ctx"), None, None), P()),
        check_vma=False,
    )
```

```python
import functools
import math

import jax
import jax.numpy as jnp
from jax import lax
from jax.experimental import pallas as pl
from jax.experimental.pallas import tpu as pltpu
from jax.sharding import PartitionSpec as P

HEADS = 8
CLIPS = 3
QUAD = 4
TILE = 8
EARLY = 3
VMEM_BYTES = 16 * 1024 * 1024
WHOLE_VMEM_BYTES = 60 * 1024 * 1024


def dot_nn(a, b):
    return lax.dot_general(a, b, (((1,), (0,)), ((), ())), preferred_element_type=jnp.float32)


def dot_nt(a, b):
    return lax.dot_general(a, b, (((1,), (1,)), ((), ())), preferred_element_type=jnp.float32)


def dot_tn(a, b):
    return lax.dot_general(a, b, (((0,), (0,)), ((), ())), preferred_element_type=jnp.float32)


def standardize(block):
    values = block.astype(jnp.float32)
    centered = values - jnp.mean(values, axis=-1, keepdims=True)
    inverse = lax.rsqrt(jnp.mean(centered * centered, axis=-1, keepdims=True) + 1e-05)
    return centered * inverse, inverse


def to_quads(first, second):
    low = lax.broadcasted_iota(jnp.int32, first.shape, 1) < QUAD
    even = jnp.where(low, first, pltpu.roll(second, QUAD, 1))
    odd = jnp.where(low, pltpu.roll(first, QUAD, 1), second)
    return even, odd


def pack_kernel(low, high, x_ref, cot_ref, w_ref, out_ref):
    _, patches, d = x_ref.shape
    homes = out_ref.shape[0] // (TILE * (high - low))

    def rows(ref):
        even, odd = to_quads(*[ref[f].astype(jnp.float32).reshape(patches // TILE, TILE, d) for f in range(2)])
        per_home = patches // homes // TILE
        found = [
            (even, odd)[q % 2][home * per_home + q // 2] for home in range(homes) for q in range(low, high)
        ]
        return jnp.concatenate(found, axis=0).astype(jnp.bfloat16)

    out_ref[:, :d] = rows(x_ref)
    out_ref[:, d:] = dot_nt(rows(cot_ref), w_ref[...]).astype(jnp.bfloat16)


def attend_kernel(
    quads, clip_ref, block, gain_ref, w_hbm, out_ref, partial_ref,
    w_ref, w_sems, standard, inverses, normed, bias, query_all, key_all, value_all, cot_all,
    probs_all, grads_all, weights_all, d_scores_all, d_query, d_key, d_value, joined, d_norm,
):
    d = w_ref.shape[1]
    inner = block.shape[1] - d
    loads = [
        pltpu.make_async_copy(
            w_hbm.at[pl.ds(part * inner, inner)], w_ref.at[pl.ds(part * inner, inner)], w_sems.at[part]
        )
        for part in range(3)
    ]
    for load in loads:
        load.start()
    wide = query_all.shape[2]
    rows = bias.shape[0]
    sources = rows // TILE
    head = inner // HEADS
    scale = 1.0 / math.sqrt(head)
    step = 8 // (1 + quads // 2)
    size = step * quads * TILE
    gains = gain_ref[...].reshape(1, d)
    frames = rows // QUAD
    begins = [sum((clip_ref[0, f] < clip).astype(jnp.int32) for f in range(frames)) for clip in range(1, CLIPS)]

    def related(dim):
        at = lax.broadcasted_iota(jnp.int32, (rows, rows), dim)
        frame, patch = at // QUAD, at % QUAD
        return sum((frame >= begin).astype(jnp.int32) for begin in begins) * QUAD + patch

    bias[...] = jnp.where(related(0) == related(1), 0.0, -1e30)

    def norm_step(i, carry):
        at = pl.ds(pl.multiple_of(i * size, size), size)
        xhat, inverse = standardize(block[at, :d])
        standard[at, :] = xhat
        inverses[at, :] = jnp.broadcast_to(inverse, (size, 128))
        normed[at, :] = (xhat * gains).astype(jnp.bfloat16)
        return carry

    lax.fori_loop(0, sources // step, norm_step, 0)

    def spread(target, found):
        found = found.reshape(sources, quads * TILE, inner)
        for q in range(quads):
            part = found[:, q * TILE : (q + 1) * TILE, :].reshape(rows, inner)
            target[q, :, :inner] = part.astype(jnp.bfloat16)
            target[q, :, inner:] = jnp.zeros((rows, wide - inner), jnp.bfloat16)

    for part, target in enumerate((query_all, key_all, value_all)):
        loads[part].wait()
        spread(target, dot_nt(normed[...], w_ref[part * inner : (part + 1) * inner, :]))
    spread(cot_all, block[:, d:].astype(jnp.float32))

    spans = []
    for h in range(HEADS):
        low = (h * head) // 128 * 128
        spans.append((low, min(-(-((h + 1) * head) // 128) * 128, wide)))

    def only(h, values):
        lanes = lax.broadcasted_iota(jnp.int32, values.shape, 1) + spans[h][0]
        return jnp.where((lanes >= h * head) & (lanes < (h + 1) * head), values, jnp.zeros_like(values))

    def quad_step(q, carry):
        for h, (low, high) in enumerate(spans):
            probs_all[h] = dot_nt(key_all[q, :, low:high], only(h, query_all[q, :, low:high]))
            grads_all[h] = dot_nt(value_all[q, :, low:high], only(h, cot_all[q, :, low:high]))
        for h in range(HEADS):
            scores = probs_all[h] * scale + bias[...]
            expo = jnp.exp(scores - jnp.max(scores, axis=0, keepdims=True))
            probs = expo * (1.0 / jnp.sum(expo, axis=0, keepdims=True))
            weights_all[h] = probs.astype(jnp.bfloat16)
            d_weights = grads_all[h]
            d_scores = probs * (d_weights - jnp.sum(probs * d_weights, axis=0, keepdims=True))
            d_scores_all[h] = d_scores.astype(jnp.bfloat16)
        at = pl.ds(pl.multiple_of(q * rows, rows), rows)
        for part, target in enumerate((d_query, d_key, d_value)):
            done = 0
            for h, (low, high) in enumerate(spans):
                if part == 0:
                    found = dot_tn(d_scores_all[h], only(h, key_all[q, :, low:high])) * scale
                elif part == 1:
                    found = dot_nn(d_scores_all[h], only(h, query_all[q, :, low:high])) * scale
                else:
                    found = dot_nn(weights_all[h], only(h, cot_all[q, :, low:high]))
                shared = max(done - low, 0)
                if shared:
                    target[:, low:done] += found[:, :shared]
                if high > done:
                    target[:, max(low, done) : high] = found[:, shared:]
                done = high
            joined[at, part * inner : (part + 1) * inner] = target[:, :inner].astype(jnp.bfloat16)
        return carry

    lax.fori_loop(0, quads, quad_step, 0)
    d_norm[...] = dot_nn(joined[...], w_ref[...]).reshape(quads, rows, d)
    partial_ref[...] = jnp.zeros_like(partial_ref)

    def back_step(i, carry):
        at = pl.ds(pl.multiple_of(i * size, size), size)
        xhat = standard[at, :]
        inverse = inverses[at, :1]
        found = d_norm[:, pl.ds(pl.multiple_of(i * step * TILE, step * TILE), step * TILE), :]
        grads = jnp.concatenate(
            [found[q, s * TILE : (s + 1) * TILE] for s in range(step) for q in range(quads)], axis=0
        )
        partial_ref[...] += jnp.sum(grads * xhat, axis=0, keepdims=True)
        e = grads * gains
        first = jnp.mean(e, axis=-1, keepdims=True)
        second = jnp.mean(e * xhat, axis=-1, keepdims=True)
        term = inverse * (e - first - xhat * second)
        out_ref[at, :] = term.astype(jnp.bfloat16)
        return carry

    lax.fori_loop(0, sources // step, back_step, 0)


def finish_kernel(cot_ref, early_ref, late_ref, out_ref, sum_ref):
    _, patches, d = cot_ref.shape
    late_rows = late_ref.shape[0]
    homes = late_rows // TILE
    early = early_ref[...].astype(jnp.float32).reshape(homes, -1, d)
    late = late_ref[...].astype(jnp.float32).reshape(homes, TILE, -1)
    term = jnp.concatenate([early, late[:, :, :d]], axis=1).reshape(patches // TILE, 2 * TILE, d)
    terms = to_quads(term[:, :TILE], term[:, TILE:])
    for f in range(2):
        total = cot_ref[f].astype(jnp.float32) + terms[f].reshape(patches, d)
        out_ref[f] = total.astype(jnp.bfloat16)

    @pl.when(pl.program_id(0) == 0)
    def _():
        sum_ref[...] = jnp.zeros_like(sum_ref)

    sum_ref[...] += jnp.sum(late[:, :, d:], axis=0)


def vmem(count):
    return [pl.BlockSpec(memory_space=pltpu.VMEM)] * count


def params(limit):
    return pltpu.CompilerParams(vmem_limit_bytes=limit)


def pack(low, high, frames, cotangent, w_out, members):
    each, patches, d = frames.shape
    inner = w_out.shape[0]
    steps = 2
    rows = members * (high - low) * TILE
    tokens = pl.BlockSpec((each, patches // steps, d), lambda i: (0, i, 0))
    return pl.pallas_call(
        functools.partial(pack_kernel, low, high),
        grid=(steps,),
        out_shape=jax.ShapeDtypeStruct((rows, d + inner), jnp.bfloat16),
        in_specs=[tokens, tokens, pl.BlockSpec((inner, d), lambda i: (0, 0))],
        out_specs=pl.BlockSpec((rows // steps, d + inner), lambda i: (i, 0)),
        compiler_params=params(WHOLE_VMEM_BYTES),
        cost_estimate=pl.CostEstimate(
            flops=2 * rows * d * inner, bytes_accessed=2 * (d * inner + 4 * rows * d), transcendentals=0
        ),
        name=f"pack_{low}",
    )(frames, cotangent, w_out)


def attend(block, clip_ids, gain, weight):
    d = weight.shape[1]
    inner = weight.shape[0] // 3
    wide = -(-inner // 128) * 128
    rows = clip_ids.shape[1] * QUAD
    quads = block.shape[0] // rows
    bf16, f32 = jnp.bfloat16, jnp.float32
    return pl.pallas_call(
        functools.partial(attend_kernel, quads),
        out_shape=(jax.ShapeDtypeStruct((quads * rows, d), bf16), jax.ShapeDtypeStruct((1, d), f32)),
        in_specs=[pl.BlockSpec(memory_space=pltpu.SMEM)] + vmem(2) + [pl.BlockSpec(memory_space=pl.ANY)],
        out_specs=tuple(vmem(2)),
        scratch_shapes=[pltpu.VMEM((3 * inner, d), bf16), pltpu.SemaphoreType.DMA((3,))]
        + [pltpu.VMEM((quads * rows, d), f32), pltpu.VMEM((quads * rows, 128), f32)]
        + [pltpu.VMEM((quads * rows, d), bf16), pltpu.VMEM((rows, rows), f32)]
        + [pltpu.VMEM((quads, rows, wide), bf16)] * 4
        + [pltpu.VMEM((HEADS, rows, rows), f32)] * 2
        + [pltpu.VMEM((HEADS, rows, rows), bf16)] * 2
        + [pltpu.VMEM((rows, wide), f32)] * 3
        + [pltpu.VMEM((quads * rows, 3 * inner), bf16), pltpu.VMEM((quads, rows, d), f32)],
        compiler_params=params(WHOLE_VMEM_BYTES),
        cost_estimate=pl.CostEstimate(flops=0, bytes_accessed=0, transcendentals=0),
        name=f"attend_{quads}",
    )(clip_ids, block, gain, weight)


def finish(cotangent, early, late):
    each, patches, d = cotangent.shape
    steps = 4
    tokens = pl.BlockSpec((each, patches // steps, d), lambda i: (0, i, 0))
    extra = late.shape[1] - d
    return pl.pallas_call(
        finish_kernel,
        grid=(steps,),
        out_shape=(
            jax.ShapeDtypeStruct(cotangent.shape, jnp.bfloat16),
            jax.ShapeDtypeStruct((TILE, extra), jnp.float32),
        ),
        in_specs=[tokens]
        + [pl.BlockSpec((rows.shape[0] // steps, rows.shape[1]), lambda i: (i, 0)) for rows in (early, late)],
        out_specs=(tokens, pl.BlockSpec((TILE, extra), lambda i: (0, 0))),
        compiler_params=params(VMEM_BYTES),
        name="finish",
    )(cotangent, early, late)


def ride(vector):
    high = lax.reduce_precision(vector, 8, 7)
    top, rest = high.reshape(-1, 128), (vector - high).reshape(-1, 128)
    over = top.shape[0] - TILE
    gap = jnp.zeros((TILE - 2 * over, 128), jnp.float32)
    middle = jnp.concatenate([top[TILE:], rest[TILE:], gap], axis=0)
    return jnp.concatenate([top[:TILE], middle, rest[:TILE]], axis=1).astype(jnp.bfloat16)


def alight(found, size):
    over = size // 128 - TILE
    first, middle, last = found[:, :128], found[:, 128:256], found[:, 256:]
    return jnp.concatenate([first + last, middle[:over] + middle[over : 2 * over]], axis=0).reshape(size)


def to_all(block):
    return lax.all_to_all(block, "ctx", 0, 0, tiled=True)


def on_device(frames, cotangent, clip_ids, gain, query_key_value_weight, w_out):
    groups = lax.axis_size("dp")
    members = lax.axis_size("ctx")
    count = groups * members * frames.shape[0] * frames.shape[1]
    d = frames.shape[2]
    quads = frames.shape[1] // members // QUAD
    weight = query_key_value_weight.T
    early = to_all(pack(0, EARLY, frames, cotangent, w_out, members))
    late = pack(EARLY, quads, frames, cotangent, w_out, members)
    early, late = lax.optimization_barrier((early, late))
    late = to_all(late)
    early_term, early_partial = attend(early, clip_ids, gain, weight)
    early_back = to_all(early_term)
    late_term, late_partial = attend(late, clip_ids, gain, weight)
    over_groups = ride(jnp.sum(lax.all_gather(early_partial + late_partial, "dp"), axis=0) * (1.0 / math.sqrt(count)))
    late_term = jnp.concatenate([late_term, jnp.tile(over_groups, (members, 1))], axis=1)
    early_back, late_term = lax.optimization_barrier((early_back, late_term))
    frame_input_gradient, total = finish(cotangent, early_back, to_all(late_term))
    return (frame_input_gradient, alight(total, d))


def solution(mesh):
    return jax.shard_map(
        on_device,
        mesh=mesh,
        in_specs=(
            P(("dp", "ctx"), None, None),
            P(("dp", "ctx"), None, None),
            P("dp", None),
            P(),
            P(),
            P(),
        ),
        out_specs=(P(("dp", "ctx"), None, None), P()),
        check_vma=False,
    )
```

```python
import functools
import math

import jax
import jax.numpy as jnp
from jax import lax
from jax.experimental import pallas as pl
from jax.experimental.pallas import tpu as pltpu
from jax.sharding import PartitionSpec as P

HEADS = 8
CLIPS = 3
QUAD = 4
TILE = 8
PIECES = 4
RIDER = 384
EARLY = 3
VMEM_BYTES = 16 * 1024 * 1024
WHOLE_VMEM_BYTES = 60 * 1024 * 1024


def dot_nn(a, b):
    return lax.dot_general(a, b, (((1,), (0,)), ((), ())), preferred_element_type=jnp.float32)


def dot_nt(a, b):
    return lax.dot_general(a, b, (((1,), (1,)), ((), ())), preferred_element_type=jnp.float32)


def dot_tn(a, b):
    return lax.dot_general(a, b, (((0,), (0,)), ((), ())), preferred_element_type=jnp.float32)


def standardize(block):
    values = block.astype(jnp.float32)
    centered = values - jnp.mean(values, axis=-1, keepdims=True)
    inverse = lax.rsqrt(jnp.mean(centered * centered, axis=-1, keepdims=True) + 1e-05)
    return centered * inverse, inverse


def to_quads(first, second):
    low = lax.broadcasted_iota(jnp.int32, first.shape, 1) < QUAD
    even = jnp.where(low, first, pltpu.roll(second, QUAD, 1))
    odd = jnp.where(low, pltpu.roll(first, QUAD, 1), second)
    return even, odd


def pack_kernel(low, high, x_ref, cot_ref, w_ref, out_ref):
    _, patches, d = x_ref.shape
    homes = out_ref.shape[0] // (TILE * (high - low))

    def rows(ref):
        even, odd = to_quads(*[ref[f].astype(jnp.float32).reshape(patches // TILE, TILE, d) for f in range(2)])
        per_home = patches // homes // TILE
        found = [
            (even, odd)[q % 2][home * per_home + q // 2] for home in range(homes) for q in range(low, high)
        ]
        return jnp.concatenate(found, axis=0).astype(jnp.bfloat16)

    out_ref[:, :d] = rows(x_ref)
    out_ref[:, d:] = dot_nt(rows(cot_ref), w_ref[...]).astype(jnp.bfloat16)


def attend_kernel(
    quads, clip_ref, block, gain_ref, before_ref, w_hbm, out_ref, partial_ref,
    w_ref, w_sems, standard, inverses, normed, bias, query_all, key_all, value_all, cot_all,
    probs_all, grads_all, weights_all, d_scores_all, d_query, d_key, d_value, joined, d_norm,
):
    d = w_ref.shape[1]
    inner = block.shape[1] - d
    piece = inner // PIECES
    loads = [
        pltpu.make_async_copy(w_hbm.at[pl.ds(k * piece, piece)], w_ref.at[pl.ds(k * piece, piece)], w_sems.at[k])
        for k in range(3 * PIECES)
    ]
    for load in loads:
        load.start()
    wide = query_all.shape[2]
    rows = bias.shape[0]
    sources = rows // TILE
    head = inner // HEADS
    scale = 1.0 / math.sqrt(head)
    step = 8 // (1 + quads // 2)
    size = step * quads * TILE
    gains = gain_ref[...].reshape(1, d)
    frames = rows // QUAD
    begins = [sum((clip_ref[0, f] < clip).astype(jnp.int32) for f in range(frames)) for clip in range(1, CLIPS)]

    def related(dim):
        at = lax.broadcasted_iota(jnp.int32, (rows, rows), dim)
        frame, patch = at // QUAD, at % QUAD
        return sum((frame >= begin).astype(jnp.int32) for begin in begins) * QUAD + patch

    bias[...] = jnp.where(related(0) == related(1), 0.0, -1e30)

    def norm_step(i, carry):
        at = pl.ds(pl.multiple_of(i * size, size), size)
        xhat, inverse = standardize(block[at, :d])
        standard[at, :] = xhat
        inverses[at, :] = jnp.broadcast_to(inverse, (size, 128))
        normed[at, :] = (xhat * gains).astype(jnp.bfloat16)
        return carry

    lax.fori_loop(0, sources // step, norm_step, 0)

    def spread(target, found):
        found = found.reshape(sources, quads * TILE, inner)
        for q in range(quads):
            part = found[:, q * TILE : (q + 1) * TILE, :].reshape(rows, inner)
            target[q, :, :inner] = part.astype(jnp.bfloat16)
            target[q, :, inner:] = jnp.zeros((rows, wide - inner), jnp.bfloat16)

    for part, target in enumerate((query_all, key_all, value_all)):
        for load in loads[part * PIECES : (part + 1) * PIECES]:
            load.wait()
        spread(target, dot_nt(normed[...], w_ref[part * inner : (part + 1) * inner, :]))
    spread(cot_all, block[:, d:].astype(jnp.float32))

    spans = []
    for h in range(HEADS):
        low = (h * head) // 128 * 128
        spans.append((low, min(-(-((h + 1) * head) // 128) * 128, wide)))

    def only(h, values):
        lanes = lax.broadcasted_iota(jnp.int32, values.shape, 1) + spans[h][0]
        return jnp.where((lanes >= h * head) & (lanes < (h + 1) * head), values, jnp.zeros_like(values))

    def quad_step(q, carry):
        for h, (low, high) in enumerate(spans):
            probs_all[h] = dot_nt(key_all[q, :, low:high], only(h, query_all[q, :, low:high]))
            grads_all[h] = dot_nt(value_all[q, :, low:high], only(h, cot_all[q, :, low:high]))
        for h in range(HEADS):
            scores = probs_all[h] * scale + bias[...]
            expo = jnp.exp(scores - jnp.max(scores, axis=0, keepdims=True))
            probs = expo * (1.0 / jnp.sum(expo, axis=0, keepdims=True))
            weights_all[h] = probs.astype(jnp.bfloat16)
            d_weights = grads_all[h]
            d_scores = probs * (d_weights - jnp.sum(probs * d_weights, axis=0, keepdims=True))
            d_scores_all[h] = d_scores.astype(jnp.bfloat16)
        at = pl.ds(pl.multiple_of(q * rows, rows), rows)
        for part, target in enumerate((d_query, d_key, d_value)):
            done = 0
            for h, (low, high) in enumerate(spans):
                if part == 0:
                    found = dot_tn(d_scores_all[h], only(h, key_all[q, :, low:high])) * scale
                elif part == 1:
                    found = dot_nn(d_scores_all[h], only(h, query_all[q, :, low:high])) * scale
                else:
                    found = dot_nn(weights_all[h], only(h, cot_all[q, :, low:high]))
                shared = max(done - low, 0)
                if shared:
                    target[:, low:done] += found[:, :shared]
                if high > done:
                    target[:, max(low, done) : high] = found[:, shared:]
                done = high
            joined[at, part * inner : (part + 1) * inner] = target[:, :inner].astype(jnp.bfloat16)
        return carry

    lax.fori_loop(0, quads, quad_step, 0)
    d_norm[...] = dot_nn(joined[...], w_ref[...]).reshape(quads, rows, d)
    partial_ref[...] = before_ref[...]
    extra = out_ref.shape[1] - d
    if extra:
        out_ref[:, d:] = jnp.zeros((out_ref.shape[0], extra), jnp.bfloat16)

    def back_step(i, carry):
        at = pl.ds(pl.multiple_of(i * size, size), size)
        xhat = standard[at, :]
        inverse = inverses[at, :1]
        found = d_norm[:, pl.ds(pl.multiple_of(i * step * TILE, step * TILE), step * TILE), :]
        grads = jnp.concatenate(
            [found[q, s * TILE : (s + 1) * TILE] for s in range(step) for q in range(quads)], axis=0
        )
        partial_ref[...] += jnp.sum(grads * xhat, axis=0, keepdims=True)
        e = grads * gains
        first = jnp.mean(e, axis=-1, keepdims=True)
        second = jnp.mean(e * xhat, axis=-1, keepdims=True)
        term = inverse * (e - first - xhat * second)
        out_ref[at, :d] = term.astype(jnp.bfloat16)
        return carry

    lax.fori_loop(0, sources // step, back_step, 0)


def finish_kernel(cot_ref, early_ref, late_ref, out_ref, sum_ref):
    _, patches, d = cot_ref.shape
    late_rows = late_ref.shape[0]
    homes = late_rows // TILE
    early = early_ref[...].astype(jnp.float32).reshape(homes, -1, d)
    late = late_ref[...].astype(jnp.float32).reshape(homes, TILE, -1)
    term = jnp.concatenate([early, late[:, :, :d]], axis=1).reshape(patches // TILE, 2 * TILE, d)
    terms = to_quads(term[:, :TILE], term[:, TILE:])
    for f in range(2):
        total = cot_ref[f].astype(jnp.float32) + terms[f].reshape(patches, d)
        out_ref[f] = total.astype(jnp.bfloat16)

    @pl.when(pl.program_id(0) == 0)
    def _():
        sum_ref[...] = jnp.zeros_like(sum_ref)

    sum_ref[...] += jnp.sum(late[:, :, d:], axis=0)


def vmem(count):
    return [pl.BlockSpec(memory_space=pltpu.VMEM)] * count


def params(limit):
    return pltpu.CompilerParams(vmem_limit_bytes=limit)


def pack(low, high, frames, cotangent, w_out, members):
    each, patches, d = frames.shape
    inner = w_out.shape[0]
    steps = 2
    rows = members * (high - low) * TILE
    tokens = pl.BlockSpec((each, patches // steps, d), lambda i: (0, i, 0))
    return pl.pallas_call(
        functools.partial(pack_kernel, low, high),
        grid=(steps,),
        out_shape=jax.ShapeDtypeStruct((rows, d + inner), jnp.bfloat16),
        in_specs=[tokens, tokens, pl.BlockSpec((inner, d), lambda i: (0, 0))],
        out_specs=pl.BlockSpec((rows // steps, d + inner), lambda i: (i, 0)),
        compiler_params=params(WHOLE_VMEM_BYTES),
        cost_estimate=pl.CostEstimate(
            flops=2 * rows * d * inner, bytes_accessed=2 * (d * inner + 4 * rows * d), transcendentals=0
        ),
        name=f"pack_{low}",
    )(frames, cotangent, w_out)


def attend(block, clip_ids, gain, weight, before, extra):
    d = weight.shape[1]
    inner = weight.shape[0] // 3
    wide = -(-inner // 128) * 128
    rows = clip_ids.shape[1] * QUAD
    quads = block.shape[0] // rows
    bf16, f32 = jnp.bfloat16, jnp.float32
    return pl.pallas_call(
        functools.partial(attend_kernel, quads),
        out_shape=(jax.ShapeDtypeStruct((quads * rows, d + extra), bf16), jax.ShapeDtypeStruct((1, d), f32)),
        in_specs=[pl.BlockSpec(memory_space=pltpu.SMEM)] + vmem(3) + [pl.BlockSpec(memory_space=pl.ANY)],
        out_specs=tuple(vmem(2)),
        scratch_shapes=[pltpu.VMEM((3 * inner, d), bf16), pltpu.SemaphoreType.DMA((3 * PIECES,))]
        + [pltpu.VMEM((quads * rows, d), f32), pltpu.VMEM((quads * rows, 128), f32)]
        + [pltpu.VMEM((quads * rows, d), bf16), pltpu.VMEM((rows, rows), f32)]
        + [pltpu.VMEM((quads, rows, wide), bf16)] * 4
        + [pltpu.VMEM((HEADS, rows, rows), f32)] * 2
        + [pltpu.VMEM((HEADS, rows, rows), bf16)] * 2
        + [pltpu.VMEM((rows, wide), f32)] * 3
        + [pltpu.VMEM((quads * rows, 3 * inner), bf16), pltpu.VMEM((quads, rows, d), f32)],
        compiler_params=params(WHOLE_VMEM_BYTES),
        cost_estimate=pl.CostEstimate(flops=0, bytes_accessed=0, transcendentals=0),
        name=f"attend_{quads}",
    )(clip_ids, block, gain, before, weight)


def finish(cotangent, early, late):
    each, patches, d = cotangent.shape
    steps = 4
    tokens = pl.BlockSpec((each, patches // steps, d), lambda i: (0, i, 0))
    extra = late.shape[1] - d
    return pl.pallas_call(
        finish_kernel,
        grid=(steps,),
        out_shape=(
            jax.ShapeDtypeStruct(cotangent.shape, jnp.bfloat16),
            jax.ShapeDtypeStruct((TILE, extra), jnp.float32),
        ),
        in_specs=[tokens]
        + [pl.BlockSpec((rows.shape[0] // steps, rows.shape[1]), lambda i: (i, 0)) for rows in (early, late)],
        out_specs=(tokens, pl.BlockSpec((TILE, extra), lambda i: (0, 0))),
        compiler_params=params(VMEM_BYTES),
        name="finish",
    )(cotangent, early, late)


def ride(vector):
    high = lax.reduce_precision(vector, 8, 7)
    top, rest = high.reshape(-1, 128), (vector - high).reshape(-1, 128)
    over = top.shape[0] - TILE
    gap = jnp.zeros((TILE - 2 * over, 128), jnp.float32)
    middle = jnp.concatenate([top[TILE:], rest[TILE:], gap], axis=0)
    return jnp.concatenate([top[:TILE], middle, rest[:TILE]], axis=1).astype(jnp.bfloat16)


def alight(found, size):
    over = size // 128 - TILE
    first, middle, last = found[:, :128], found[:, 128:256], found[:, 256:]
    return jnp.concatenate([first + last, middle[:over] + middle[over : 2 * over]], axis=0).reshape(size)


def to_all(block):
    return lax.all_to_all(block, "ctx", 0, 0, tiled=True)


def sum_groups(value, groups):
    side = math.isqrt(groups)
    if side * side != groups:
        return lax.psum(value, "dp")
    rows = [[i * side + j for j in range(side)] for i in range(side)]
    value = lax.psum(value, "dp", axis_index_groups=rows)
    moved = [lax.ppermute(value, "dp", [(i, (i + k * side) % groups) for i in range(groups)]) for k in range(1, side)]
    return functools.reduce(jnp.add, moved, value)


def on_device(frames, cotangent, clip_ids, gain, query_key_value_weight, w_out):
    groups = lax.axis_size("dp")
    members = lax.axis_size("ctx")
    count = groups * members * frames.shape[0] * frames.shape[1]
    d = frames.shape[2]
    quads = frames.shape[1] // members // QUAD
    weight = query_key_value_weight.T
    early = to_all(pack(0, EARLY, frames, cotangent, w_out, members))
    late = pack(EARLY, quads, frames, cotangent, w_out, members)
    early, late = lax.optimization_barrier((early, late))
    late = to_all(late)
    early_term, partial_term = attend(early, clip_ids, gain, weight, jnp.zeros((1, d), jnp.float32), 0)
    early_back = to_all(early_term)
    late_term, partial_term = attend(late, clip_ids, gain, weight, partial_term, RIDER)
    rider = ride(sum_groups(partial_term, groups) * (1.0 / math.sqrt(count)))
    late_term = lax.dynamic_update_slice(late_term, jnp.tile(rider, (members, 1)), (0, d))
    early_back, late_term = lax.optimization_barrier((early_back, late_term))
    frame_input_gradient, total = finish(cotangent, early_back, to_all(late_term))
    return (frame_input_gradient, alight(total, d))


def solution(mesh):
    return jax.shard_map(
        on_device,
        mesh=mesh,
        in_specs=(
            P(("dp", "ctx"), None, None),
            P(("dp", "ctx"), None, None),
            P("dp", None),
            P(),
            P(),
            P(),
        ),
        out_specs=(P(("dp", "ctx"), None, None), P()),
        check_vma=False,
    )
```

```python
import functools
import math

import jax
import jax.numpy as jnp
from jax import lax
from jax.experimental import pallas as pl
from jax.experimental.pallas import tpu as pltpu
from jax.sharding import PartitionSpec as P

HEADS = 8
CLIPS = 3
QUAD = 4
TILE = 8
PIECES = 4
RIDER = 384
EARLY = 3
VMEM_BYTES = 16 * 1024 * 1024
WHOLE_VMEM_BYTES = 60 * 1024 * 1024


def dot_nn(a, b):
    return lax.dot_general(a, b, (((1,), (0,)), ((), ())), preferred_element_type=jnp.float32)


def dot_nt(a, b):
    return lax.dot_general(a, b, (((1,), (1,)), ((), ())), preferred_element_type=jnp.float32)


def dot_tn(a, b):
    return lax.dot_general(a, b, (((0,), (0,)), ((), ())), preferred_element_type=jnp.float32)


def standardize(block):
    values = block.astype(jnp.float32)
    centered = values - jnp.mean(values, axis=-1, keepdims=True)
    inverse = lax.rsqrt(jnp.mean(centered * centered, axis=-1, keepdims=True) + 1e-05)
    return centered * inverse, inverse


def to_quads(first, second):
    low = lax.broadcasted_iota(jnp.int32, first.shape, 1) < QUAD
    even = jnp.where(low, first, pltpu.roll(second, QUAD, 1))
    odd = jnp.where(low, pltpu.roll(first, QUAD, 1), second)
    return even, odd


def pack_kernel(low, high, x_ref, cot_ref, w_ref, out_ref):
    _, patches, d = x_ref.shape
    homes = out_ref.shape[0] // (TILE * (high - low))

    def rows(ref):
        even, odd = to_quads(*[ref[f].astype(jnp.float32).reshape(patches // TILE, TILE, d) for f in range(2)])
        per_home = patches // homes // TILE
        found = [
            (even, odd)[q % 2][home * per_home + q // 2] for home in range(homes) for q in range(low, high)
        ]
        return jnp.concatenate(found, axis=0).astype(jnp.bfloat16)

    out_ref[:, :d] = rows(x_ref)
    out_ref[:, d:] = dot_nt(rows(cot_ref), w_ref[...]).astype(jnp.bfloat16)


def late_kernel(quads, clip_ref, block, gain_ref, w_hbm, before_ref, *refs):
    attend_kernel(quads, clip_ref, block, gain_ref, w_hbm, *refs, before_ref=before_ref)


def attend_kernel(
    quads, clip_ref, block, gain_ref, w_hbm, out_ref, partial_ref,
    w_ref, w_sems, standard, inverses, normed, bias, query_all, key_all, value_all, cot_all,
    probs_all, grads_all, weights_all, d_scores_all, d_query, d_key, d_value, joined, d_norm, before_ref=None,
):
    d = w_ref.shape[1]
    inner = block.shape[1] - d
    piece = inner // PIECES
    loads = [
        pltpu.make_async_copy(w_hbm.at[pl.ds(k * piece, piece)], w_ref.at[pl.ds(k * piece, piece)], w_sems.at[k])
        for k in range(3 * PIECES)
    ]
    for load in loads:
        load.start()
    wide = query_all.shape[2]
    rows = bias.shape[0]
    sources = rows // TILE
    head = inner // HEADS
    scale = 1.0 / math.sqrt(head)
    step = 8 // (1 + quads // 2)
    size = step * quads * TILE
    gains = gain_ref[...].reshape(1, d)
    frames = rows // QUAD
    begins = [sum((clip_ref[0, f] < clip).astype(jnp.int32) for f in range(frames)) for clip in range(1, CLIPS)]

    def related(dim):
        at = lax.broadcasted_iota(jnp.int32, (rows, rows), dim)
        frame, patch = at // QUAD, at % QUAD
        return sum((frame >= begin).astype(jnp.int32) for begin in begins) * QUAD + patch

    bias[...] = jnp.where(related(0) == related(1), 0.0, -1e30)

    def norm_step(i, carry):
        at = pl.ds(pl.multiple_of(i * size, size), size)
        xhat, inverse = standardize(block[at, :d])
        standard[at, :] = xhat
        inverses[at, :] = jnp.broadcast_to(inverse, (size, 128))
        normed[at, :] = (xhat * gains).astype(jnp.bfloat16)
        return carry

    lax.fori_loop(0, sources // step, norm_step, 0)

    def spread(target, found):
        found = found.reshape(sources, quads * TILE, inner)
        for q in range(quads):
            part = found[:, q * TILE : (q + 1) * TILE, :].reshape(rows, inner)
            target[q, :, :inner] = part.astype(jnp.bfloat16)
            target[q, :, inner:] = jnp.zeros((rows, wide - inner), jnp.bfloat16)

    spread(cot_all, block[:, d:].astype(jnp.float32))
    for part, target in enumerate((query_all, key_all, value_all)):
        for load in loads[part * PIECES : (part + 1) * PIECES]:
            load.wait()
        spread(target, dot_nt(normed[...], w_ref[part * inner : (part + 1) * inner, :]))
    spans = []
    for h in range(HEADS):
        low = (h * head) // 128 * 128
        spans.append((low, min(-(-((h + 1) * head) // 128) * 128, wide)))

    def only(h, values):
        lanes = lax.broadcasted_iota(jnp.int32, values.shape, 1) + spans[h][0]
        return jnp.where((lanes >= h * head) & (lanes < (h + 1) * head), values, jnp.zeros_like(values))

    def quad_step(q, carry):
        for h, (low, high) in enumerate(spans):
            probs_all[h] = dot_nt(key_all[q, :, low:high], only(h, query_all[q, :, low:high]))
            grads_all[h] = dot_nt(value_all[q, :, low:high], only(h, cot_all[q, :, low:high]))
        for h in range(HEADS):
            scores = probs_all[h] * scale + bias[...]
            expo = jnp.exp(scores - jnp.max(scores, axis=0, keepdims=True))
            probs = expo * (1.0 / jnp.sum(expo, axis=0, keepdims=True))
            weights_all[h] = probs.astype(jnp.bfloat16)
            d_weights = grads_all[h]
            d_scores = probs * (d_weights - jnp.sum(probs * d_weights, axis=0, keepdims=True))
            d_scores_all[h] = d_scores.astype(jnp.bfloat16)
        at = pl.ds(pl.multiple_of(q * rows, rows), rows)
        for part, target in enumerate((d_query, d_key, d_value)):
            done = 0
            for h, (low, high) in enumerate(spans):
                if part == 0:
                    found = dot_tn(d_scores_all[h], only(h, key_all[q, :, low:high])) * scale
                elif part == 1:
                    found = dot_nn(d_scores_all[h], only(h, query_all[q, :, low:high])) * scale
                else:
                    found = dot_nn(weights_all[h], only(h, cot_all[q, :, low:high]))
                shared = max(done - low, 0)
                if shared:
                    target[:, low:done] += found[:, :shared]
                if high > done:
                    target[:, max(low, done) : high] = found[:, shared:]
                done = high
            joined[at, part * inner : (part + 1) * inner] = target[:, :inner].astype(jnp.bfloat16)
        return carry

    lax.fori_loop(0, quads, quad_step, 0)
    d_norm[...] = dot_nn(joined[...], w_ref[...]).reshape(quads, rows, d)
    partial_ref[...] = jnp.zeros_like(partial_ref) if before_ref is None else before_ref[...]
    extra = out_ref.shape[1] - d
    if extra:
        out_ref[:, d:] = jnp.zeros((out_ref.shape[0], extra), jnp.bfloat16)

    def back_step(i, carry):
        at = pl.ds(pl.multiple_of(i * size, size), size)
        xhat = standard[at, :]
        inverse = inverses[at, :1]
        found = d_norm[:, pl.ds(pl.multiple_of(i * step * TILE, step * TILE), step * TILE), :]
        grads = jnp.concatenate(
            [found[q, s * TILE : (s + 1) * TILE] for s in range(step) for q in range(quads)], axis=0
        )
        partial_ref[...] += jnp.sum(grads * xhat, axis=0, keepdims=True)
        e = grads * gains
        first = jnp.mean(e, axis=-1, keepdims=True)
        second = jnp.mean(e * xhat, axis=-1, keepdims=True)
        term = inverse * (e - first - xhat * second)
        out_ref[at, :d] = term.astype(jnp.bfloat16)
        return carry

    lax.fori_loop(0, sources // step, back_step, 0)


def finish_kernel(cot_ref, early_ref, late_ref, out_ref, sum_ref, rider):
    _, patches, d = cot_ref.shape
    late_rows = late_ref.shape[0]
    homes = late_rows // TILE
    early = early_ref[...].astype(jnp.float32).reshape(homes, -1, d)
    late = late_ref[...].astype(jnp.float32).reshape(homes, TILE, -1)
    term = jnp.concatenate([early, late[:, :, :d]], axis=1).reshape(patches // TILE, 2 * TILE, d)
    terms = to_quads(term[:, :TILE], term[:, TILE:])
    for f in range(2):
        total = cot_ref[f].astype(jnp.float32) + terms[f].reshape(patches, d)
        out_ref[f] = total.astype(jnp.bfloat16)

    @pl.when(pl.program_id(0) == 0)
    def _():
        rider[...] = jnp.zeros_like(rider)

    rider[...] += jnp.sum(late[:, :, d:], axis=0)

    @pl.when(pl.program_id(0) == pl.num_programs(0) - 1)
    def _():
        over = d // 128 - TILE
        for row in range(d // 128):
            if row < TILE:
                both = rider[row, :128] + rider[row, 256:]
            else:
                both = rider[row - TILE, 128:256] + rider[row - TILE + over, 128:256]
            sum_ref[row * 128 : (row + 1) * 128] = both


def vmem(count):
    return [pl.BlockSpec(memory_space=pltpu.VMEM)] * count


def params(limit):
    return pltpu.CompilerParams(vmem_limit_bytes=limit)


def pack(low, high, frames, cotangent, w_out, members):
    each, patches, d = frames.shape
    inner = w_out.shape[0]
    steps = 2
    rows = members * (high - low) * TILE
    tokens = pl.BlockSpec((each, patches // steps, d), lambda i: (0, i, 0))
    return pl.pallas_call(
        functools.partial(pack_kernel, low, high),
        grid=(steps,),
        out_shape=jax.ShapeDtypeStruct((rows, d + inner), jnp.bfloat16),
        in_specs=[tokens, tokens, pl.BlockSpec((inner, d), lambda i: (0, 0))],
        out_specs=pl.BlockSpec((rows // steps, d + inner), lambda i: (i, 0)),
        compiler_params=params(WHOLE_VMEM_BYTES),
        cost_estimate=pl.CostEstimate(
            flops=2 * rows * d * inner, bytes_accessed=2 * (d * inner + 4 * rows * d), transcendentals=0
        ),
        name=f"pack_{low}",
    )(frames, cotangent, w_out)


def attend(block, clip_ids, gain, weight, before=None, extra=0):
    d = weight.shape[1]
    inner = weight.shape[0] // 3
    wide = -(-inner // 128) * 128
    rows = clip_ids.shape[1] * QUAD
    quads = block.shape[0] // rows
    bf16, f32 = jnp.bfloat16, jnp.float32
    more = [] if before is None else [before]
    return pl.pallas_call(
        functools.partial(late_kernel if more else attend_kernel, quads),
        out_shape=(jax.ShapeDtypeStruct((quads * rows, d + extra), bf16), jax.ShapeDtypeStruct((1, d), f32)),
        in_specs=[pl.BlockSpec(memory_space=pltpu.SMEM)] + vmem(2) + [pl.BlockSpec(memory_space=pl.ANY)] + vmem(len(more)),
        out_specs=tuple(vmem(2)),
        scratch_shapes=[pltpu.VMEM((3 * inner, d), bf16), pltpu.SemaphoreType.DMA((3 * PIECES,))]
        + [pltpu.VMEM((quads * rows, d), f32), pltpu.VMEM((quads * rows, 128), f32)]
        + [pltpu.VMEM((quads * rows, d), bf16), pltpu.VMEM((rows, rows), f32)]
        + [pltpu.VMEM((quads, rows, wide), bf16)] * 4
        + [pltpu.VMEM((HEADS, rows, rows), f32)] * 2
        + [pltpu.VMEM((HEADS, rows, rows), bf16)] * 2
        + [pltpu.VMEM((rows, wide), f32)] * 3
        + [pltpu.VMEM((quads * rows, 3 * inner), bf16), pltpu.VMEM((quads, rows, d), f32)],
        compiler_params=params(WHOLE_VMEM_BYTES),
        cost_estimate=pl.CostEstimate(flops=0, bytes_accessed=0, transcendentals=0),
        name=f"attend_{quads}",
    )(clip_ids, block, gain, weight, *more)


def finish(cotangent, early, late):
    each, patches, d = cotangent.shape
    steps = 2
    tokens = pl.BlockSpec((each, patches // steps, d), lambda i: (0, i, 0))
    extra = late.shape[1] - d
    return pl.pallas_call(
        finish_kernel,
        grid=(steps,),
        out_shape=(
            jax.ShapeDtypeStruct(cotangent.shape, jnp.bfloat16),
            jax.ShapeDtypeStruct((d,), jnp.float32),
        ),
        in_specs=[tokens]
        + [pl.BlockSpec((rows.shape[0] // steps, rows.shape[1]), lambda i: (i, 0)) for rows in (early, late)],
        out_specs=(tokens, pl.BlockSpec((d,), lambda i: (0,))),
        scratch_shapes=[pltpu.VMEM((TILE, extra), jnp.float32)],
        compiler_params=params(VMEM_BYTES),
        name="finish",
    )(cotangent, early, late)


def ride(vector):
    high = lax.reduce_precision(vector, 8, 7)
    top, rest = high.reshape(-1, 128), (vector - high).reshape(-1, 128)
    over = top.shape[0] - TILE
    gap = jnp.zeros((TILE - 2 * over, 128), jnp.float32)
    middle = jnp.concatenate([top[TILE:], rest[TILE:], gap], axis=0)
    return jnp.concatenate([top[:TILE], middle, rest[:TILE]], axis=1).astype(jnp.bfloat16)


def to_all(block):
    return lax.all_to_all(block, "ctx", 0, 0, tiled=True)


def sum_groups(value, groups):
    side = math.isqrt(groups)
    if side * side != groups:
        return lax.psum(value, "dp")
    rows = [[i * side + j for j in range(side)] for i in range(side)]
    value = lax.psum(value, "dp", axis_index_groups=rows)
    moved = [lax.ppermute(value, "dp", [(i, (i + k * side) % groups) for i in range(groups)]) for k in range(1, side)]
    return functools.reduce(jnp.add, moved, value)


def on_device(frames, cotangent, clip_ids, gain, query_key_value_weight, w_out):
    groups = lax.axis_size("dp")
    members = lax.axis_size("ctx")
    count = groups * members * frames.shape[0] * frames.shape[1]
    d = frames.shape[2]
    quads = frames.shape[1] // members // QUAD
    weight = query_key_value_weight.T
    early = to_all(pack(0, EARLY, frames, cotangent, w_out, members))
    late = pack(EARLY, quads, frames, cotangent, w_out, members)
    early, late = lax.optimization_barrier((early, late))
    late = to_all(late)
    early_term, partial_term = attend(early, clip_ids, gain, weight)
    early_back = to_all(early_term)
    late_term, partial_term = attend(late, clip_ids, gain, weight, partial_term, RIDER)
    rider = ride(sum_groups(partial_term, groups) * (1.0 / math.sqrt(count)))
    late_term = lax.dynamic_update_slice(late_term, jnp.tile(rider, (members, 1)), (0, d))
    early_back, late_term = lax.optimization_barrier((early_back, late_term))
    return finish(cotangent, early_back, to_all(late_term))


def solution(mesh):
    return jax.shard_map(
        on_device,
        mesh=mesh,
        in_specs=(
            P(("dp", "ctx"), None, None),
            P(("dp", "ctx"), None, None),
            P("dp", None),
            P(),
            P(),
            P(),
        ),
        out_specs=(P(("dp", "ctx"), None, None), P()),
        check_vma=False,
    )
```

```python
import functools
import math

import jax
import jax.numpy as jnp
from jax import lax
from jax.experimental import pallas as pl
from jax.experimental.pallas import tpu as pltpu
from jax.sharding import PartitionSpec as P

HEADS = 8
CLIPS = 3
QUAD = 4
TILE = 8
PIECES = 4
RIDER = 384
EARLY = 3
VMEM_BYTES = 16 * 1024 * 1024
WHOLE_VMEM_BYTES = 60 * 1024 * 1024


def dot_nn(a, b):
    return lax.dot_general(a, b, (((1,), (0,)), ((), ())), preferred_element_type=jnp.float32)


def dot_nt(a, b):
    return lax.dot_general(a, b, (((1,), (1,)), ((), ())), preferred_element_type=jnp.float32)


def dot_tn(a, b):
    return lax.dot_general(a, b, (((0,), (0,)), ((), ())), preferred_element_type=jnp.float32)


def standardize(block):
    values = block.astype(jnp.float32)
    centered = values - jnp.mean(values, axis=-1, keepdims=True)
    inverse = lax.rsqrt(jnp.mean(centered * centered, axis=-1, keepdims=True) + 1e-05)
    return centered * inverse, inverse


def to_quads(first, second):
    low = lax.broadcasted_iota(jnp.int32, first.shape, 1) < QUAD
    even = jnp.where(low, first, pltpu.roll(second, QUAD, 1))
    odd = jnp.where(low, pltpu.roll(first, QUAD, 1), second)
    return even, odd


def pack_kernel(low, high, x_hbm, cot_hbm, w_hbm, out_hbm, x_ref, cot_ref, w_ref, out_ref, load_sems, store_sems):
    _, patches, d = x_ref.shape
    total = out_ref.shape[0]
    homes = total // (TILE * (high - low))
    per_home = patches // homes // TILE
    loads = [
        pltpu.make_async_copy(source, target, load_sems.at[k])
        for k, (source, target) in enumerate(((cot_hbm, cot_ref), (w_hbm, w_ref), (x_hbm, x_ref)))
    ]
    for load in loads:
        load.start()

    def rows(ref, part, parts):
        size = patches // parts
        block = [ref[f, part * size : (part + 1) * size].astype(jnp.float32) for f in range(2)]
        even, odd = to_quads(*[values.reshape(size // TILE, TILE, d) for values in block])
        found = [
            (even, odd)[q % 2][home * per_home + q // 2] for home in range(homes // parts) for q in range(low, high)
        ]
        return jnp.concatenate(found, axis=0).astype(jnp.bfloat16)

    loads[0].wait()
    cot = rows(cot_ref, 0, 1)
    loads[1].wait()
    out_ref[:, d:] = dot_nt(cot, w_ref[...]).astype(jnp.bfloat16)
    loads[2].wait()
    half = total // 2
    stores = []
    for part in range(2):
        at = pl.ds(part * half, half)
        out_ref[at, :d] = rows(x_ref, part, 2)
        stores.append(pltpu.make_async_copy(out_ref.at[at], out_hbm.at[at], store_sems.at[part]))
        stores[part].start()
    for store in stores:
        store.wait()


def late_kernel(quads, clip_ref, block, gain_ref, w_hbm, before_ref, *refs):
    attend_kernel(quads, clip_ref, block, gain_ref, w_hbm, *refs, before_ref=before_ref)


def attend_kernel(
    quads, clip_ref, block, gain_ref, w_hbm, out_ref, partial_ref,
    w_ref, w_sems, standard, inverses, normed, bias, query_all, key_all, value_all, cot_all,
    probs_all, grads_all, weights_all, d_scores_all, d_query, d_key, d_value, joined, d_norm, before_ref=None,
):
    d = w_ref.shape[1]
    inner = block.shape[1] - d
    piece = inner // PIECES
    loads = [
        pltpu.make_async_copy(w_hbm.at[pl.ds(k * piece, piece)], w_ref.at[pl.ds(k * piece, piece)], w_sems.at[k])
        for k in range(3 * PIECES)
    ]
    for load in loads:
        load.start()
    wide = query_all.shape[2]
    rows = bias.shape[0]
    sources = rows // TILE
    head = inner // HEADS
    scale = 1.0 / math.sqrt(head)
    step = 8 // (1 + quads // 2)
    size = step * quads * TILE
    gains = gain_ref[...].reshape(1, d)
    frames = rows // QUAD
    begins = [sum((clip_ref[0, f] < clip).astype(jnp.int32) for f in range(frames)) for clip in range(1, CLIPS)]

    def related(dim):
        at = lax.broadcasted_iota(jnp.int32, (rows, rows), dim)
        frame, patch = at // QUAD, at % QUAD
        return sum((frame >= begin).astype(jnp.int32) for begin in begins) * QUAD + patch

    bias[...] = jnp.where(related(0) == related(1), 0.0, -1e30)

    def norm_step(i, carry):
        at = pl.ds(pl.multiple_of(i * size, size), size)
        xhat, inverse = standardize(block[at, :d])
        standard[at, :] = xhat
        inverses[at, :] = jnp.broadcast_to(inverse, (size, 128))
        normed[at, :] = (xhat * gains).astype(jnp.bfloat16)
        return carry

    lax.fori_loop(0, sources // step, norm_step, 0)

    def spread(target, found):
        found = found.reshape(sources, quads * TILE, inner)
        for q in range(quads):
            part = found[:, q * TILE : (q + 1) * TILE, :].reshape(rows, inner)
            target[q, :, :inner] = part.astype(jnp.bfloat16)
            target[q, :, inner:] = jnp.zeros((rows, wide - inner), jnp.bfloat16)

    spread(cot_all, block[:, d:].astype(jnp.float32))
    for part, target in enumerate((query_all, key_all, value_all)):
        for load in loads[part * PIECES : (part + 1) * PIECES]:
            load.wait()
        spread(target, dot_nt(normed[...], w_ref[part * inner : (part + 1) * inner, :]))
    spans = []
    for h in range(HEADS):
        low = (h * head) // 128 * 128
        spans.append((low, min(-(-((h + 1) * head) // 128) * 128, wide)))

    def only(h, values):
        lanes = lax.broadcasted_iota(jnp.int32, values.shape, 1) + spans[h][0]
        return jnp.where((lanes >= h * head) & (lanes < (h + 1) * head), values, jnp.zeros_like(values))

    def quad_step(q, carry):
        for h, (low, high) in enumerate(spans):
            probs_all[h] = dot_nt(key_all[q, :, low:high], only(h, query_all[q, :, low:high]))
            grads_all[h] = dot_nt(value_all[q, :, low:high], only(h, cot_all[q, :, low:high]))
        for h in range(HEADS):
            scores = probs_all[h] * scale + bias[...]
            expo = jnp.exp(scores - jnp.max(scores, axis=0, keepdims=True))
            probs = expo * (1.0 / jnp.sum(expo, axis=0, keepdims=True))
            weights_all[h] = probs.astype(jnp.bfloat16)
            d_weights = grads_all[h]
            d_scores = probs * (d_weights - jnp.sum(probs * d_weights, axis=0, keepdims=True))
            d_scores_all[h] = d_scores.astype(jnp.bfloat16)
        at = pl.ds(pl.multiple_of(q * rows, rows), rows)
        for part, target in enumerate((d_query, d_key, d_value)):
            done = 0
            for h, (low, high) in enumerate(spans):
                if part == 0:
                    found = dot_tn(d_scores_all[h], only(h, key_all[q, :, low:high])) * scale
                elif part == 1:
                    found = dot_nn(d_scores_all[h], only(h, query_all[q, :, low:high])) * scale
                else:
                    found = dot_nn(weights_all[h], only(h, cot_all[q, :, low:high]))
                shared = max(done - low, 0)
                if shared:
                    target[:, low:done] += found[:, :shared]
                if high > done:
                    target[:, max(low, done) : high] = found[:, shared:]
                done = high
            joined[at, part * inner : (part + 1) * inner] = target[:, :inner].astype(jnp.bfloat16)
        return carry

    lax.fori_loop(0, quads, quad_step, 0)
    d_norm[...] = dot_nn(joined[...], w_ref[...]).reshape(quads, rows, d)
    partial_ref[...] = jnp.zeros_like(partial_ref) if before_ref is None else before_ref[...]
    extra = out_ref.shape[1] - d
    if extra:
        out_ref[:, d:] = jnp.zeros((out_ref.shape[0], extra), jnp.bfloat16)

    def back_step(i, carry):
        at = pl.ds(pl.multiple_of(i * size, size), size)
        xhat = standard[at, :]
        inverse = inverses[at, :1]
        found = d_norm[:, pl.ds(pl.multiple_of(i * step * TILE, step * TILE), step * TILE), :]
        grads = jnp.concatenate(
            [found[q, s * TILE : (s + 1) * TILE] for s in range(step) for q in range(quads)], axis=0
        )
        partial_ref[...] += jnp.sum(grads * xhat, axis=0, keepdims=True)
        e = grads * gains
        first = jnp.mean(e, axis=-1, keepdims=True)
        second = jnp.mean(e * xhat, axis=-1, keepdims=True)
        term = inverse * (e - first - xhat * second)
        out_ref[at, :d] = term.astype(jnp.bfloat16)
        return carry

    lax.fori_loop(0, sources // step, back_step, 0)


def finish_kernel(cot_ref, early_ref, late_ref, out_ref, sum_ref, rider):
    _, patches, d = cot_ref.shape
    late_rows = late_ref.shape[0]
    homes = late_rows // TILE
    early = early_ref[...].astype(jnp.float32).reshape(homes, -1, d)
    late = late_ref[...].astype(jnp.float32).reshape(homes, TILE, -1)
    term = jnp.concatenate([early, late[:, :, :d]], axis=1).reshape(patches // TILE, 2 * TILE, d)
    terms = to_quads(term[:, :TILE], term[:, TILE:])
    for f in range(2):
        total = cot_ref[f].astype(jnp.float32) + terms[f].reshape(patches, d)
        out_ref[f] = total.astype(jnp.bfloat16)

    @pl.when(pl.program_id(0) == 0)
    def _():
        rider[...] = jnp.zeros_like(rider)

    rider[...] += jnp.sum(late[:, :, d:], axis=0)

    @pl.when(pl.program_id(0) == pl.num_programs(0) - 1)
    def _():
        over = d // 128 - TILE
        for row in range(d // 128):
            if row < TILE:
                both = rider[row, :128] + rider[row, 256:]
            else:
                both = rider[row - TILE, 128:256] + rider[row - TILE + over, 128:256]
            sum_ref[row * 128 : (row + 1) * 128] = both


def vmem(count):
    return [pl.BlockSpec(memory_space=pltpu.VMEM)] * count


def params(limit):
    return pltpu.CompilerParams(vmem_limit_bytes=limit)


def pack(low, high, frames, cotangent, w_out, members):
    inner, d = w_out.shape
    rows = members * (high - low) * TILE
    anywhere = pl.BlockSpec(memory_space=pl.ANY)
    return pl.pallas_call(
        functools.partial(pack_kernel, low, high),
        out_shape=jax.ShapeDtypeStruct((rows, d + inner), jnp.bfloat16),
        in_specs=[anywhere] * 3,
        out_specs=anywhere,
        scratch_shapes=[
            pltpu.VMEM(frames.shape, jnp.bfloat16),
            pltpu.VMEM(cotangent.shape, jnp.bfloat16),
            pltpu.VMEM(w_out.shape, jnp.bfloat16),
            pltpu.VMEM((rows, d + inner), jnp.bfloat16),
            pltpu.SemaphoreType.DMA((3,)),
            pltpu.SemaphoreType.DMA((2,)),
        ],
        compiler_params=params(WHOLE_VMEM_BYTES),
        cost_estimate=pl.CostEstimate(
            flops=2 * rows * d * inner, bytes_accessed=2 * (d * inner + 4 * rows * d), transcendentals=0
        ),
        name=f"pack_{low}",
    )(frames, cotangent, w_out)


def attend(block, clip_ids, gain, weight, before=None, extra=0):
    d = weight.shape[1]
    inner = weight.shape[0] // 3
    wide = -(-inner // 128) * 128
    rows = clip_ids.shape[1] * QUAD
    quads = block.shape[0] // rows
    bf16, f32 = jnp.bfloat16, jnp.float32
    more = [] if before is None else [before]
    return pl.pallas_call(
        functools.partial(late_kernel if more else attend_kernel, quads),
        out_shape=(jax.ShapeDtypeStruct((quads * rows, d + extra), bf16), jax.ShapeDtypeStruct((1, d), f32)),
        in_specs=[pl.BlockSpec(memory_space=pltpu.SMEM)] + vmem(2) + [pl.BlockSpec(memory_space=pl.ANY)] + vmem(len(more)),
        out_specs=tuple(vmem(2)),
        scratch_shapes=[pltpu.VMEM((3 * inner, d), bf16), pltpu.SemaphoreType.DMA((3 * PIECES,))]
        + [pltpu.VMEM((quads * rows, d), f32), pltpu.VMEM((quads * rows, 128), f32)]
        + [pltpu.VMEM((quads * rows, d), bf16), pltpu.VMEM((rows, rows), f32)]
        + [pltpu.VMEM((quads, rows, wide), bf16)] * 4
        + [pltpu.VMEM((HEADS, rows, rows), f32)] * 2
        + [pltpu.VMEM((HEADS, rows, rows), bf16)] * 2
        + [pltpu.VMEM((rows, wide), f32)] * 3
        + [pltpu.VMEM((quads * rows, 3 * inner), bf16), pltpu.VMEM((quads, rows, d), f32)],
        compiler_params=params(WHOLE_VMEM_BYTES),
        cost_estimate=pl.CostEstimate(flops=0, bytes_accessed=0, transcendentals=0),
        name=f"attend_{quads}",
    )(clip_ids, block, gain, weight, *more)


def finish(cotangent, early, late):
    each, patches, d = cotangent.shape
    steps = 2
    tokens = pl.BlockSpec((each, patches // steps, d), lambda i: (0, i, 0))
    extra = late.shape[1] - d
    return pl.pallas_call(
        finish_kernel,
        grid=(steps,),
        out_shape=(
            jax.ShapeDtypeStruct(cotangent.shape, jnp.bfloat16),
            jax.ShapeDtypeStruct((d,), jnp.float32),
        ),
        in_specs=[tokens]
        + [pl.BlockSpec((rows.shape[0] // steps, rows.shape[1]), lambda i: (i, 0)) for rows in (early, late)],
        out_specs=(tokens, pl.BlockSpec((d,), lambda i: (0,))),
        scratch_shapes=[pltpu.VMEM((TILE, extra), jnp.float32)],
        compiler_params=params(VMEM_BYTES),
        name="finish",
    )(cotangent, early, late)


def ride(vector):
    high = lax.reduce_precision(vector, 8, 7)
    top, rest = high.reshape(-1, 128), (vector - high).reshape(-1, 128)
    over = top.shape[0] - TILE
    gap = jnp.zeros((TILE - 2 * over, 128), jnp.float32)
    middle = jnp.concatenate([top[TILE:], rest[TILE:], gap], axis=0)
    return jnp.concatenate([top[:TILE], middle, rest[:TILE]], axis=1).astype(jnp.bfloat16)


def to_all(block):
    return lax.all_to_all(block, "ctx", 0, 0, tiled=True)


def sum_groups(value, groups):
    side = math.isqrt(groups)
    if side * side != groups:
        return lax.psum(value, "dp")
    rows = [[i * side + j for j in range(side)] for i in range(side)]
    value = lax.psum(value, "dp", axis_index_groups=rows)
    moved = [lax.ppermute(value, "dp", [(i, (i + k * side) % groups) for i in range(groups)]) for k in range(1, side)]
    return functools.reduce(jnp.add, moved, value)


def on_device(frames, cotangent, clip_ids, gain, query_key_value_weight, w_out):
    groups = lax.axis_size("dp")
    members = lax.axis_size("ctx")
    count = groups * members * frames.shape[0] * frames.shape[1]
    d = frames.shape[2]
    quads = frames.shape[1] // members // QUAD
    weight = query_key_value_weight.T
    early = to_all(pack(0, EARLY, frames, cotangent, w_out, members))
    late = pack(EARLY, quads, frames, cotangent, w_out, members)
    early, late = lax.optimization_barrier((early, late))
    late = to_all(late)
    early_term, partial_term = attend(early, clip_ids, gain, weight)
    early_back = to_all(early_term)
    late_term, partial_term = attend(late, clip_ids, gain, weight, partial_term, RIDER)
    rider = ride(sum_groups(partial_term, groups) * (1.0 / math.sqrt(count)))
    late_term = lax.dynamic_update_slice(late_term, jnp.tile(rider, (members, 1)), (0, d))
    early_back, late_term = lax.optimization_barrier((early_back, late_term))
    return finish(cotangent, early_back, to_all(late_term))


def solution(mesh):
    return jax.shard_map(
        on_device,
        mesh=mesh,
        in_specs=(
            P(("dp", "ctx"), None, None),
            P(("dp", "ctx"), None, None),
            P("dp", None),
            P(),
            P(),
            P(),
        ),
        out_specs=(P(("dp", "ctx"), None, None), P()),
        check_vma=False,
    )
```

```python
import functools
import math

import jax
import jax.numpy as jnp
from jax import lax
from jax.experimental import pallas as pl
from jax.experimental.pallas import tpu as pltpu
from jax.sharding import PartitionSpec as P

HEADS = 8
CLIPS = 3
QUAD = 4
TILE = 8
PIECES = 4
RIDER = 384
EARLY = 3
VMEM_BYTES = 16 * 1024 * 1024
WHOLE_VMEM_BYTES = 60 * 1024 * 1024


def dot_nn(a, b):
    return lax.dot_general(a, b, (((1,), (0,)), ((), ())), preferred_element_type=jnp.float32)


def dot_nt(a, b):
    return lax.dot_general(a, b, (((1,), (1,)), ((), ())), preferred_element_type=jnp.float32)


def dot_tn(a, b):
    return lax.dot_general(a, b, (((0,), (0,)), ((), ())), preferred_element_type=jnp.float32)


def standardize(block):
    values = block.astype(jnp.float32)
    centered = values - jnp.mean(values, axis=-1, keepdims=True)
    inverse = lax.rsqrt(jnp.mean(centered * centered, axis=-1, keepdims=True) + 1e-05)
    return centered * inverse, inverse


def to_quads(first, second):
    low = lax.broadcasted_iota(jnp.int32, first.shape, 1) < QUAD
    even = jnp.where(low, first, pltpu.roll(second, QUAD, 1))
    odd = jnp.where(low, pltpu.roll(first, QUAD, 1), second)
    return even, odd


def pack_kernel(low, high, x_hbm, cot_hbm, w_hbm, out_hbm, x_ref, cot_ref, w_ref, out_ref, load_sems, store_sems):
    _, patches, d = x_ref.shape
    total = out_ref.shape[0]
    homes = total // (TILE * (high - low))
    per_home = patches // homes // TILE
    loads = [
        pltpu.make_async_copy(source, target, load_sems.at[k])
        for k, (source, target) in enumerate(((cot_hbm, cot_ref), (w_hbm, w_ref), (x_hbm, x_ref)))
    ]
    for load in loads:
        load.start()

    def rows(ref, part, parts):
        size = patches // parts
        block = [ref[f, part * size : (part + 1) * size].astype(jnp.float32) for f in range(2)]
        even, odd = to_quads(*[values.reshape(size // TILE, TILE, d) for values in block])
        found = [
            (even, odd)[q % 2][home * per_home + q // 2] for home in range(homes // parts) for q in range(low, high)
        ]
        return jnp.concatenate(found, axis=0).astype(jnp.bfloat16)

    loads[0].wait()
    cot = rows(cot_ref, 0, 1)
    loads[1].wait()
    out_ref[:, d:] = dot_nt(cot, w_ref[...]).astype(jnp.bfloat16)
    loads[2].wait()
    half = total // 2
    stores = []
    for part in range(2):
        at = pl.ds(part * half, half)
        out_ref[at, :d] = rows(x_ref, part, 2)
        stores.append(pltpu.make_async_copy(out_ref.at[at], out_hbm.at[at], store_sems.at[part]))
        stores[part].start()
    for store in stores:
        store.wait()


def late_kernel(quads, clip_ref, block, gain_ref, w_hbm, before_ref, *refs):
    attend_kernel(quads, clip_ref, block, gain_ref, w_hbm, *refs, before_ref=before_ref)


def attend_kernel(
    quads, clip_ref, block, gain_ref, w_hbm, out_ref, partial_ref,
    w_ref, w_sems, standard, inverses, normed, bias, query_all, key_all, value_all, cot_all,
    probs_all, grads_all, weights_all, d_scores_all, d_query, d_key, d_value, joined, d_norm, before_ref=None,
):
    d = w_ref.shape[1]
    inner = block.shape[1] - d
    piece = inner // PIECES
    loads = [
        pltpu.make_async_copy(w_hbm.at[pl.ds(k * piece, piece)], w_ref.at[pl.ds(k * piece, piece)], w_sems.at[k])
        for k in range(3 * PIECES)
    ]
    for load in loads:
        load.start()
    wide = query_all.shape[2]
    rows = bias.shape[0]
    sources = rows // TILE
    head = inner // HEADS
    scale = 1.0 / math.sqrt(head)
    step = 8 // (1 + quads // 2)
    size = step * quads * TILE
    gains = gain_ref[...].reshape(1, d)
    frames = rows // QUAD
    begins = [sum((clip_ref[0, f] < clip).astype(jnp.int32) for f in range(frames)) for clip in range(1, CLIPS)]

    def related(dim):
        at = lax.broadcasted_iota(jnp.int32, (rows, rows), dim)
        frame, patch = at // QUAD, at % QUAD
        return sum((frame >= begin).astype(jnp.int32) for begin in begins) * QUAD + patch

    bias[...] = jnp.where(related(0) == related(1), 0.0, -1e30)

    def norm_step(i, carry):
        at = pl.ds(pl.multiple_of(i * size, size), size)
        xhat, inverse = standardize(block[at, :d])
        standard[at, :] = xhat
        inverses[at, :] = jnp.broadcast_to(inverse, (size, 128))
        normed[at, :] = (xhat * gains).astype(jnp.bfloat16)
        return carry

    lax.fori_loop(0, sources // step, norm_step, 0)

    def spread(target, found):
        found = found.reshape(sources, quads * TILE, inner)
        for q in range(quads):
            part = found[:, q * TILE : (q + 1) * TILE, :].reshape(rows, inner)
            target[q, :, :inner] = part.astype(jnp.bfloat16)
            target[q, :, inner:] = jnp.zeros((rows, wide - inner), jnp.bfloat16)

    spread(cot_all, block[:, d:].astype(jnp.float32))
    for part, target in enumerate((query_all, key_all, value_all)):
        for load in loads[part * PIECES : (part + 1) * PIECES]:
            load.wait()
        spread(target, dot_nt(normed[...], w_ref[part * inner : (part + 1) * inner, :]))
    spans = []
    for h in range(HEADS):
        low = (h * head) // 128 * 128
        spans.append((low, min(-(-((h + 1) * head) // 128) * 128, wide)))

    def only(h, values):
        lanes = lax.broadcasted_iota(jnp.int32, values.shape, 1) + spans[h][0]
        return jnp.where((lanes >= h * head) & (lanes < (h + 1) * head), values, jnp.zeros_like(values))

    def quad_step(q, carry):
        for h, (low, high) in enumerate(spans):
            probs_all[h] = dot_nt(key_all[q, :, low:high], only(h, query_all[q, :, low:high]))
            grads_all[h] = dot_nt(value_all[q, :, low:high], only(h, cot_all[q, :, low:high]))
        for h in range(HEADS):
            scores = probs_all[h] * scale + bias[...]
            expo = jnp.exp(scores - jnp.max(scores, axis=0, keepdims=True))
            probs = expo * (1.0 / jnp.sum(expo, axis=0, keepdims=True))
            weights_all[h] = probs.astype(jnp.bfloat16)
            d_weights = grads_all[h]
            d_scores = probs * (d_weights - jnp.sum(probs * d_weights, axis=0, keepdims=True))
            d_scores_all[h] = d_scores.astype(jnp.bfloat16)
        at = pl.ds(pl.multiple_of(q * rows, rows), rows)
        for part, target in enumerate((d_query, d_key, d_value)):
            done = 0
            for h, (low, high) in enumerate(spans):
                if part == 0:
                    found = dot_tn(d_scores_all[h], only(h, key_all[q, :, low:high])) * scale
                elif part == 1:
                    found = dot_nn(d_scores_all[h], only(h, query_all[q, :, low:high])) * scale
                else:
                    found = dot_nn(weights_all[h], only(h, cot_all[q, :, low:high]))
                shared = max(done - low, 0)
                if shared:
                    target[:, low:done] += found[:, :shared]
                if high > done:
                    target[:, max(low, done) : high] = found[:, shared:]
                done = high
            joined[at, part * inner : (part + 1) * inner] = target[:, :inner].astype(jnp.bfloat16)
        return carry

    lax.fori_loop(0, quads, quad_step, 0)
    d_norm[...] = dot_nn(joined[...], w_ref[...]).reshape(quads, rows, d)
    partial_ref[...] = jnp.zeros_like(partial_ref) if before_ref is None else before_ref[...]
    extra = out_ref.shape[1] - d
    if extra:
        out_ref[:, d:] = jnp.zeros((out_ref.shape[0], extra), jnp.bfloat16)

    def back_step(i, carry):
        at = pl.ds(pl.multiple_of(i * size, size), size)
        xhat = standard[at, :]
        inverse = inverses[at, :1]
        found = d_norm[:, pl.ds(pl.multiple_of(i * step * TILE, step * TILE), step * TILE), :]
        grads = jnp.concatenate(
            [found[q, s * TILE : (s + 1) * TILE] for s in range(step) for q in range(quads)], axis=0
        )
        partial_ref[...] += jnp.sum(grads * xhat, axis=0, keepdims=True)
        e = grads * gains
        first = jnp.mean(e, axis=-1, keepdims=True)
        second = jnp.mean(e * xhat, axis=-1, keepdims=True)
        term = inverse * (e - first - xhat * second)
        out_ref[at, :d] = term.astype(jnp.bfloat16)
        return carry

    lax.fori_loop(0, sources // step, back_step, 0)


def finish_kernel(cot_ref, early_ref, late_ref, out_hbm, sum_ref, out_ref, sems):
    _, patches, d = cot_ref.shape
    parts = sems.shape[0]
    homes = late_ref.shape[0] // TILE
    few, size = homes // parts, patches // parts
    rider = jnp.zeros((TILE, late_ref.shape[1] - d), jnp.float32)
    stores = []
    for part in range(parts):
        many = early_ref.shape[0] // parts
        early = early_ref[part * many : (part + 1) * many].astype(jnp.float32).reshape(few, -1, d)
        late = late_ref[part * few * TILE : (part + 1) * few * TILE].astype(jnp.float32).reshape(few, TILE, -1)
        term = jnp.concatenate([early, late[:, :, :d]], axis=1).reshape(size // TILE, 2 * TILE, d)
        terms = to_quads(term[:, :TILE], term[:, TILE:])
        for f in range(2):
            total = cot_ref[f, part * size : (part + 1) * size].astype(jnp.float32) + terms[f].reshape(size, d)
            out_ref[f, part * size : (part + 1) * size] = total.astype(jnp.bfloat16)
        at = pl.ds(part * size, size)
        stores.append(pltpu.make_async_copy(out_ref.at[:, at], out_hbm.at[:, at], sems.at[part]))
        stores[part].start()
        rider = rider + jnp.sum(late[:, :, d:], axis=0)
    over = d // 128 - TILE
    for row in range(d // 128):
        if row < TILE:
            both = rider[row, :128] + rider[row, 256:]
        else:
            both = rider[row - TILE, 128:256] + rider[row - TILE + over, 128:256]
        sum_ref[row * 128 : (row + 1) * 128] = both
    for store in stores:
        store.wait()


def vmem(count):
    return [pl.BlockSpec(memory_space=pltpu.VMEM)] * count


def params(limit):
    return pltpu.CompilerParams(vmem_limit_bytes=limit)


def pack(low, high, frames, cotangent, w_out, members):
    inner, d = w_out.shape
    rows = members * (high - low) * TILE
    anywhere = pl.BlockSpec(memory_space=pl.ANY)
    return pl.pallas_call(
        functools.partial(pack_kernel, low, high),
        out_shape=jax.ShapeDtypeStruct((rows, d + inner), jnp.bfloat16),
        in_specs=[anywhere] * 3,
        out_specs=anywhere,
        scratch_shapes=[
            pltpu.VMEM(frames.shape, jnp.bfloat16),
            pltpu.VMEM(cotangent.shape, jnp.bfloat16),
            pltpu.VMEM(w_out.shape, jnp.bfloat16),
            pltpu.VMEM((rows, d + inner), jnp.bfloat16),
            pltpu.SemaphoreType.DMA((3,)),
            pltpu.SemaphoreType.DMA((2,)),
        ],
        compiler_params=params(WHOLE_VMEM_BYTES),
        cost_estimate=pl.CostEstimate(
            flops=2 * rows * d * inner, bytes_accessed=2 * (d * inner + 4 * rows * d), transcendentals=0
        ),
        name=f"pack_{low}",
    )(frames, cotangent, w_out)


def attend(block, clip_ids, gain, weight, before=None, extra=0):
    d = weight.shape[1]
    inner = weight.shape[0] // 3
    wide = -(-inner // 128) * 128
    rows = clip_ids.shape[1] * QUAD
    quads = block.shape[0] // rows
    bf16, f32 = jnp.bfloat16, jnp.float32
    more = [] if before is None else [before]
    return pl.pallas_call(
        functools.partial(late_kernel if more else attend_kernel, quads),
        out_shape=(jax.ShapeDtypeStruct((quads * rows, d + extra), bf16), jax.ShapeDtypeStruct((1, d), f32)),
        in_specs=[pl.BlockSpec(memory_space=pltpu.SMEM)] + vmem(2) + [pl.BlockSpec(memory_space=pl.ANY)] + vmem(len(more)),
        out_specs=tuple(vmem(2)),
        scratch_shapes=[pltpu.VMEM((3 * inner, d), bf16), pltpu.SemaphoreType.DMA((3 * PIECES,))]
        + [pltpu.VMEM((quads * rows, d), f32), pltpu.VMEM((quads * rows, 128), f32)]
        + [pltpu.VMEM((quads * rows, d), bf16), pltpu.VMEM((rows, rows), f32)]
        + [pltpu.VMEM((quads, rows, wide), bf16)] * 4
        + [pltpu.VMEM((HEADS, rows, rows), f32)] * 2
        + [pltpu.VMEM((HEADS, rows, rows), bf16)] * 2
        + [pltpu.VMEM((rows, wide), f32)] * 3
        + [pltpu.VMEM((quads * rows, 3 * inner), bf16), pltpu.VMEM((quads, rows, d), f32)],
        compiler_params=params(WHOLE_VMEM_BYTES),
        cost_estimate=pl.CostEstimate(flops=0, bytes_accessed=0, transcendentals=0),
        name=f"attend_{quads}",
    )(clip_ids, block, gain, weight, *more)


def finish(cotangent, early, late):
    d = cotangent.shape[2]
    parts = 4
    return pl.pallas_call(
        finish_kernel,
        out_shape=(
            jax.ShapeDtypeStruct(cotangent.shape, jnp.bfloat16),
            jax.ShapeDtypeStruct((d,), jnp.float32),
        ),
        in_specs=vmem(3),
        out_specs=(pl.BlockSpec(memory_space=pl.ANY), vmem(1)[0]),
        scratch_shapes=[pltpu.VMEM(cotangent.shape, jnp.bfloat16), pltpu.SemaphoreType.DMA((parts,))],
        compiler_params=params(VMEM_BYTES),
        name="finish",
    )(cotangent, early, late)


def ride(vector):
    high = lax.reduce_precision(vector, 8, 7)
    top, rest = high.reshape(-1, 128), (vector - high).reshape(-1, 128)
    over = top.shape[0] - TILE
    gap = jnp.zeros((TILE - 2 * over, 128), jnp.float32)
    middle = jnp.concatenate([top[TILE:], rest[TILE:], gap], axis=0)
    return jnp.concatenate([top[:TILE], middle, rest[:TILE]], axis=1).astype(jnp.bfloat16)


def to_all(block):
    return lax.all_to_all(block, "ctx", 0, 0, tiled=True)


def sum_groups(value, groups):
    side = math.isqrt(groups)
    if side * side != groups:
        return lax.psum(value, "dp")
    rows = [[i * side + j for j in range(side)] for i in range(side)]
    value = lax.psum(value, "dp", axis_index_groups=rows)
    moved = [lax.ppermute(value, "dp", [(i, (i + k * side) % groups) for i in range(groups)]) for k in range(1, side)]
    return functools.reduce(jnp.add, moved, value)


def on_device(frames, cotangent, clip_ids, gain, query_key_value_weight, w_out):
    groups = lax.axis_size("dp")
    members = lax.axis_size("ctx")
    count = groups * members * frames.shape[0] * frames.shape[1]
    d = frames.shape[2]
    quads = frames.shape[1] // members // QUAD
    weight = query_key_value_weight.T
    early = to_all(pack(0, EARLY, frames, cotangent, w_out, members))
    late = pack(EARLY, quads, frames, cotangent, w_out, members)
    early, late = lax.optimization_barrier((early, late))
    late = to_all(late)
    early_term, partial_term = attend(early, clip_ids, gain, weight)
    early_back = to_all(early_term)
    late_term, partial_term = attend(late, clip_ids, gain, weight, partial_term, RIDER)
    rider = ride(sum_groups(partial_term, groups) * (1.0 / math.sqrt(count)))
    late_term = lax.dynamic_update_slice(late_term, jnp.tile(rider, (members, 1)), (0, d))
    early_back, late_term = lax.optimization_barrier((early_back, late_term))
    return finish(cotangent, early_back, to_all(late_term))


def solution(mesh):
    return jax.shard_map(
        on_device,
        mesh=mesh,
        in_specs=(
            P(("dp", "ctx"), None, None),
            P(("dp", "ctx"), None, None),
            P("dp", None),
            P(),
            P(),
            P(),
        ),
        out_specs=(P(("dp", "ctx"), None, None), P()),
        check_vma=False,
    )
```

```python
import functools
import math

import jax
import jax.numpy as jnp
from jax import lax
from jax.experimental import pallas as pl
from jax.experimental.pallas import tpu as pltpu
from jax.sharding import PartitionSpec as P

HEADS = 8
CLIPS = 3
QUAD = 4
TILE = 8
PIECES = 1
RIDER = 384
EARLY = 3
VMEM_BYTES = 16 * 1024 * 1024
WHOLE_VMEM_BYTES = 60 * 1024 * 1024


def dot_nn(a, b):
    return lax.dot_general(a, b, (((1,), (0,)), ((), ())), preferred_element_type=jnp.float32)


def dot_nt(a, b):
    return lax.dot_general(a, b, (((1,), (1,)), ((), ())), preferred_element_type=jnp.float32)


def dot_tn(a, b):
    return lax.dot_general(a, b, (((0,), (0,)), ((), ())), preferred_element_type=jnp.float32)


def standardize(block):
    values = block.astype(jnp.float32)
    centered = values - jnp.mean(values, axis=-1, keepdims=True)
    inverse = lax.rsqrt(jnp.mean(centered * centered, axis=-1, keepdims=True) + 1e-05)
    return centered * inverse, inverse


def to_quads(first, second):
    low = lax.broadcasted_iota(jnp.int32, first.shape, 1) < QUAD
    even = jnp.where(low, first, pltpu.roll(second, QUAD, 1))
    odd = jnp.where(low, pltpu.roll(first, QUAD, 1), second)
    return even, odd


def pack_kernel(low, high, x_hbm, cot_hbm, w_hbm, out_hbm, x_ref, cot_ref, w_ref, out_ref, load_sems, store_sems):
    _, patches, d = x_ref.shape
    total = out_ref.shape[0]
    homes = total // (TILE * (high - low))
    per_home = patches // homes // TILE
    loads = [
        pltpu.make_async_copy(source, target, load_sems.at[k])
        for k, (source, target) in enumerate(((cot_hbm, cot_ref), (w_hbm, w_ref), (x_hbm, x_ref)))
    ]
    for load in loads:
        load.start()

    def rows(ref, part, parts):
        size = patches // parts
        block = [ref[f, part * size : (part + 1) * size].astype(jnp.float32) for f in range(2)]
        even, odd = to_quads(*[values.reshape(size // TILE, TILE, d) for values in block])
        found = [
            (even, odd)[q % 2][home * per_home + q // 2] for home in range(homes // parts) for q in range(low, high)
        ]
        return jnp.concatenate(found, axis=0).astype(jnp.bfloat16)

    loads[0].wait()
    cot = rows(cot_ref, 0, 1)
    loads[1].wait()
    out_ref[:, d:] = dot_nt(cot, w_ref[...]).astype(jnp.bfloat16)
    loads[2].wait()
    half = total // 2
    stores = []
    for part in range(2):
        at = pl.ds(part * half, half)
        out_ref[at, :d] = rows(x_ref, part, 2)
        stores.append(pltpu.make_async_copy(out_ref.at[at], out_hbm.at[at], store_sems.at[part]))
        stores[part].start()
    for store in stores:
        store.wait()


def late_kernel(quads, clip_ref, block, gain_ref, w_hbm, before_ref, *refs):
    attend_kernel(quads, clip_ref, block, gain_ref, w_hbm, *refs, before_ref=before_ref)


def attend_kernel(
    quads, clip_ref, block, gain_ref, w_hbm, out_ref, partial_ref,
    w_ref, w_sems, standard, inverses, normed, bias, query_all, key_all, value_all, cot_all,
    probs_all, grads_all, weights_all, d_scores_all, d_query, d_key, d_value, joined, d_norm, before_ref=None,
):
    d = w_ref.shape[1]
    inner = block.shape[1] - d
    piece = inner // PIECES
    loads = [
        pltpu.make_async_copy(w_hbm.at[pl.ds(k * piece, piece)], w_ref.at[pl.ds(k * piece, piece)], w_sems.at[k])
        for k in range(3 * PIECES)
    ]
    for load in loads:
        load.start()
    wide = query_all.shape[2]
    rows = bias.shape[0]
    sources = rows // TILE
    head = inner // HEADS
    scale = 1.0 / math.sqrt(head)
    step = 8 // (1 + quads // 2)
    size = step * quads * TILE
    gains = gain_ref[...].reshape(1, d)
    frames = rows // QUAD
    begins = [sum((clip_ref[0, f] < clip).astype(jnp.int32) for f in range(frames)) for clip in range(1, CLIPS)]

    def related(dim):
        at = lax.broadcasted_iota(jnp.int32, (rows, rows), dim)
        frame, patch = at // QUAD, at % QUAD
        return sum((frame >= begin).astype(jnp.int32) for begin in begins) * QUAD + patch

    bias[...] = jnp.where(related(0) == related(1), 0.0, -1e30)

    def norm_step(i, carry):
        at = pl.ds(pl.multiple_of(i * size, size), size)
        xhat, inverse = standardize(block[at, :d])
        standard[at, :] = xhat
        inverses[at, :] = jnp.broadcast_to(inverse, (size, 128))
        normed[at, :] = (xhat * gains).astype(jnp.bfloat16)
        return carry

    lax.fori_loop(0, sources // step, norm_step, 0)

    def spread(target, found):
        found = found.reshape(sources, quads * TILE, inner)
        for q in range(quads):
            part = found[:, q * TILE : (q + 1) * TILE, :].reshape(rows, inner)
            target[q, :, :inner] = part.astype(jnp.bfloat16)
            target[q, :, inner:] = jnp.zeros((rows, wide - inner), jnp.bfloat16)

    spread(cot_all, block[:, d:].astype(jnp.float32))
    for part, target in enumerate((query_all, key_all, value_all)):
        for load in loads[part * PIECES : (part + 1) * PIECES]:
            load.wait()
        spread(target, dot_nt(normed[...], w_ref[part * inner : (part + 1) * inner, :]))
    spans = []
    for h in range(HEADS):
        low = (h * head) // 128 * 128
        spans.append((low, min(-(-((h + 1) * head) // 128) * 128, wide)))

    def only(h, values):
        lanes = lax.broadcasted_iota(jnp.int32, values.shape, 1) + spans[h][0]
        return jnp.where((lanes >= h * head) & (lanes < (h + 1) * head), values, jnp.zeros_like(values))

    def quad_step(q, carry):
        for h, (low, high) in enumerate(spans):
            probs_all[h] = dot_nt(key_all[q, :, low:high], only(h, query_all[q, :, low:high]))
            grads_all[h] = dot_nt(value_all[q, :, low:high], only(h, cot_all[q, :, low:high]))
        for h in range(HEADS):
            scores = probs_all[h] * scale + bias[...]
            expo = jnp.exp(scores - jnp.max(scores, axis=0, keepdims=True))
            probs = expo * (1.0 / jnp.sum(expo, axis=0, keepdims=True))
            weights_all[h] = probs.astype(jnp.bfloat16)
            d_weights = grads_all[h]
            d_scores = probs * (d_weights - jnp.sum(probs * d_weights, axis=0, keepdims=True))
            d_scores_all[h] = d_scores.astype(jnp.bfloat16)
        at = pl.ds(pl.multiple_of(q * rows, rows), rows)
        for part, target in enumerate((d_query, d_key, d_value)):
            done = 0
            for h, (low, high) in enumerate(spans):
                if part == 0:
                    found = dot_tn(d_scores_all[h], only(h, key_all[q, :, low:high])) * scale
                elif part == 1:
                    found = dot_nn(d_scores_all[h], only(h, query_all[q, :, low:high])) * scale
                else:
                    found = dot_nn(weights_all[h], only(h, cot_all[q, :, low:high]))
                shared = max(done - low, 0)
                if shared:
                    target[:, low:done] += found[:, :shared]
                if high > done:
                    target[:, max(low, done) : high] = found[:, shared:]
                done = high
            joined[at, part * inner : (part + 1) * inner] = target[:, :inner].astype(jnp.bfloat16)
        return carry

    lax.fori_loop(0, quads, quad_step, 0)
    d_norm[...] = dot_nn(joined[...], w_ref[...]).reshape(quads, rows, d)
    partial_ref[...] = jnp.zeros_like(partial_ref) if before_ref is None else before_ref[...]
    extra = out_ref.shape[1] - d
    if extra:
        out_ref[:, d:] = jnp.zeros((out_ref.shape[0], extra), jnp.bfloat16)

    def back_step(i, carry):
        at = pl.ds(pl.multiple_of(i * size, size), size)
        xhat = standard[at, :]
        inverse = inverses[at, :1]
        found = d_norm[:, pl.ds(pl.multiple_of(i * step * TILE, step * TILE), step * TILE), :]
        grads = jnp.concatenate(
            [found[q, s * TILE : (s + 1) * TILE] for s in range(step) for q in range(quads)], axis=0
        )
        partial_ref[...] += jnp.sum(grads * xhat, axis=0, keepdims=True)
        e = grads * gains
        first = jnp.mean(e, axis=-1, keepdims=True)
        second = jnp.mean(e * xhat, axis=-1, keepdims=True)
        term = inverse * (e - first - xhat * second)
        out_ref[at, :d] = term.astype(jnp.bfloat16)
        return carry

    lax.fori_loop(0, sources // step, back_step, 0)


def finish_kernel(cot_ref, early_ref, late_ref, out_ref, sum_ref, rider):
    _, patches, d = cot_ref.shape
    late_rows = late_ref.shape[0]
    homes = late_rows // TILE
    early = early_ref[...].astype(jnp.float32).reshape(homes, -1, d)
    late = late_ref[...].astype(jnp.float32).reshape(homes, TILE, -1)
    term = jnp.concatenate([early, late[:, :, :d]], axis=1).reshape(patches // TILE, 2 * TILE, d)
    terms = to_quads(term[:, :TILE], term[:, TILE:])
    for f in range(2):
        total = cot_ref[f].astype(jnp.float32) + terms[f].reshape(patches, d)
        out_ref[f] = total.astype(jnp.bfloat16)

    @pl.when(pl.program_id(0) == 0)
    def _():
        rider[...] = jnp.zeros_like(rider)

    rider[...] += jnp.sum(late[:, :, d:], axis=0)

    @pl.when(pl.program_id(0) == pl.num_programs(0) - 1)
    def _():
        over = d // 128 - TILE
        for row in range(d // 128):
            if row < TILE:
                both = rider[row, :128] + rider[row, 256:]
            else:
                both = rider[row - TILE, 128:256] + rider[row - TILE + over, 128:256]
            sum_ref[row * 128 : (row + 1) * 128] = both


def vmem(count):
    return [pl.BlockSpec(memory_space=pltpu.VMEM)] * count


def params(limit):
    return pltpu.CompilerParams(vmem_limit_bytes=limit)


def pack(low, high, frames, cotangent, w_out, members):
    inner, d = w_out.shape
    rows = members * (high - low) * TILE
    anywhere = pl.BlockSpec(memory_space=pl.ANY)
    return pl.pallas_call(
        functools.partial(pack_kernel, low, high),
        out_shape=jax.ShapeDtypeStruct((rows, d + inner), jnp.bfloat16),
        in_specs=[anywhere] * 3,
        out_specs=anywhere,
        scratch_shapes=[
            pltpu.VMEM(frames.shape, jnp.bfloat16),
            pltpu.VMEM(cotangent.shape, jnp.bfloat16),
            pltpu.VMEM(w_out.shape, jnp.bfloat16),
            pltpu.VMEM((rows, d + inner), jnp.bfloat16),
            pltpu.SemaphoreType.DMA((3,)),
            pltpu.SemaphoreType.DMA((2,)),
        ],
        compiler_params=params(WHOLE_VMEM_BYTES),
        cost_estimate=pl.CostEstimate(
            flops=2 * rows * d * inner, bytes_accessed=2 * (d * inner + 4 * rows * d), transcendentals=0
        ),
        name=f"pack_{low}",
    )(frames, cotangent, w_out)


def attend(block, clip_ids, gain, weight, before=None, extra=0):
    d = weight.shape[1]
    inner = weight.shape[0] // 3
    wide = -(-inner // 128) * 128
    rows = clip_ids.shape[1] * QUAD
    quads = block.shape[0] // rows
    bf16, f32 = jnp.bfloat16, jnp.float32
    more = [] if before is None else [before]
    return pl.pallas_call(
        functools.partial(late_kernel if more else attend_kernel, quads),
        out_shape=(jax.ShapeDtypeStruct((quads * rows, d + extra), bf16), jax.ShapeDtypeStruct((1, d), f32)),
        in_specs=[pl.BlockSpec(memory_space=pltpu.SMEM)] + vmem(2) + [pl.BlockSpec(memory_space=pl.ANY)] + vmem(len(more)),
        out_specs=tuple(vmem(2)),
        scratch_shapes=[pltpu.VMEM((3 * inner, d), bf16), pltpu.SemaphoreType.DMA((3 * PIECES,))]
        + [pltpu.VMEM((quads * rows, d), f32), pltpu.VMEM((quads * rows, 128), f32)]
        + [pltpu.VMEM((quads * rows, d), bf16), pltpu.VMEM((rows, rows), f32)]
        + [pltpu.VMEM((quads, rows, wide), bf16)] * 4
        + [pltpu.VMEM((HEADS, rows, rows), f32)] * 2
        + [pltpu.VMEM((HEADS, rows, rows), bf16)] * 2
        + [pltpu.VMEM((rows, wide), f32)] * 3
        + [pltpu.VMEM((quads * rows, 3 * inner), bf16), pltpu.VMEM((quads, rows, d), f32)],
        compiler_params=params(WHOLE_VMEM_BYTES),
        cost_estimate=pl.CostEstimate(flops=0, bytes_accessed=0, transcendentals=0),
        name=f"attend_{quads}",
    )(clip_ids, block, gain, weight, *more)


def finish(cotangent, early, late):
    each, patches, d = cotangent.shape
    steps = 2
    tokens = pl.BlockSpec((each, patches // steps, d), lambda i: (0, i, 0))
    extra = late.shape[1] - d
    return pl.pallas_call(
        finish_kernel,
        grid=(steps,),
        out_shape=(
            jax.ShapeDtypeStruct(cotangent.shape, jnp.bfloat16),
            jax.ShapeDtypeStruct((d,), jnp.float32),
        ),
        in_specs=[tokens]
        + [pl.BlockSpec((rows.shape[0] // steps, rows.shape[1]), lambda i: (i, 0)) for rows in (early, late)],
        out_specs=(tokens, pl.BlockSpec((d,), lambda i: (0,))),
        scratch_shapes=[pltpu.VMEM((TILE, extra), jnp.float32)],
        compiler_params=params(VMEM_BYTES),
        name="finish",
    )(cotangent, early, late)


def ride(vector):
    high = lax.reduce_precision(vector, 8, 7)
    top, rest = high.reshape(-1, 128), (vector - high).reshape(-1, 128)
    over = top.shape[0] - TILE
    gap = jnp.zeros((TILE - 2 * over, 128), jnp.float32)
    middle = jnp.concatenate([top[TILE:], rest[TILE:], gap], axis=0)
    return jnp.concatenate([top[:TILE], middle, rest[:TILE]], axis=1).astype(jnp.bfloat16)


def to_all(block):
    return lax.all_to_all(block, "ctx", 0, 0, tiled=True)


def sum_groups(value, groups):
    side = math.isqrt(groups)
    if side * side != groups:
        return lax.psum(value, "dp")
    rows = [[i * side + j for j in range(side)] for i in range(side)]
    value = lax.psum(value, "dp", axis_index_groups=rows)
    moved = [lax.ppermute(value, "dp", [(i, (i + k * side) % groups) for i in range(groups)]) for k in range(1, side)]
    return functools.reduce(jnp.add, moved, value)


def on_device(frames, cotangent, clip_ids, gain, query_key_value_weight, w_out):
    groups = lax.axis_size("dp")
    members = lax.axis_size("ctx")
    count = groups * members * frames.shape[0] * frames.shape[1]
    d = frames.shape[2]
    quads = frames.shape[1] // members // QUAD
    weight = query_key_value_weight.T
    early = to_all(pack(0, EARLY, frames, cotangent, w_out, members))
    late = pack(EARLY, quads, frames, cotangent, w_out, members)
    early, late = lax.optimization_barrier((early, late))
    late = to_all(late)
    early_term, partial_term = attend(early, clip_ids, gain, weight)
    early_back = to_all(early_term)
    late_term, partial_term = attend(late, clip_ids, gain, weight, partial_term, RIDER)
    rider = ride(sum_groups(partial_term, groups) * (1.0 / math.sqrt(count)))
    late_term = lax.dynamic_update_slice(late_term, jnp.tile(rider, (members, 1)), (0, d))
    early_back, late_term = lax.optimization_barrier((early_back, late_term))
    return finish(cotangent, early_back, to_all(late_term))


def solution(mesh):
    return jax.shard_map(
        on_device,
        mesh=mesh,
        in_specs=(
            P(("dp", "ctx"), None, None),
            P(("dp", "ctx"), None, None),
            P("dp", None),
            P(),
            P(),
            P(),
        ),
        out_specs=(P(("dp", "ctx"), None, None), P()),
        check_vma=False,
    )
```
